256 devices in a mesh: dp: 8 (over x, core), ctx: 16 (over y, z_hi), head: 2 (over z_lo).
Axes of the slice: x: 4, y: 4, z: 8 (z_hi: 4, z_lo: 2; z = z_hi * 2 + z_lo), core: 2. Of those that a mesh axis runs over, the one named last changes fastest.
Arguments:
- layer_input: bfloat16 [8, 2048, 4096], P('dp', 'ctx', 'head'), may hold values from -24 to 24
- w_step: bfloat16 [4096, 128], P('dp', 'head'), may hold values from -0.09375 to 0.09375
- step_bias: float32 [128], P('head'), may hold values from -14 to -5
- decay_rate: float32 [128], P('head'), may hold values from 1 to 8
- ssm_input: bfloat16 [8, 2048, 8192], P('dp', 'ctx', 'head'), may hold values from -6 to 6
- b_input: bfloat16 [8, 2048, 1024], P('dp', 'ctx', 'head'), may hold values from -6 to 6
- c_input: bfloat16 [8, 2048, 1024], P('dp', 'ctx', 'head'), may hold values from -0.046875 to 0.046875
- skip_gain: float32 [128], P('head'), may hold values from 0.5 to 1.5
- grad_y: bfloat16 [8, 2048, 8192], P('dp', 'ctx', 'head'), may hold values from -6 to 6
Outputs:
- output: bfloat16 [8, 2048, 8192], P('dp', 'ctx', 'head')
- grad_x: bfloat16 [8, 2048, 8192], P('dp', 'ctx', 'head')
- grad_b: bfloat16 [8, 2048, 1024], P('dp', 'ctx', 'head')
- grad_c: bfloat16 [8, 2048, 1024], P('dp', 'ctx', 'head')
- grad_input: bfloat16 [8, 2048, 4096], P('dp', 'ctx', 'head')
- grad_w_step: float32 [4096, 128], P('dp', 'head')
The draws below stay inside these ranges and needn't reach their ends.
All inputs are finite; a program needn't handle non-finite values.
Results may differ from the reference program's by a relative error of at most 0.014.
Values may be sent and summed in bfloat16 or wider, within the bound.
No kernel may reach another device: no remote copies, remote signals or barrier semaphores. Data moves between devices by JAX's collectives and lax.ppermute only.
A program may use at most 192 MiB of HBM per device.

```python
import jax
import jax.numpy as jnp
from jax import lax

D = 4096
H = 128
P_SIZE = 64
N = 128
G = 8
Q = 128
TOK_DEV = 128
SEQ = 2048
BATCH = 8


def draw_layer_input(key, part):
    key = jax.random.fold_in(key, 3)
    noise_key, spot_key, pair_key = jax.random.split(key, 3)
    base = jax.random.truncated_normal(noise_key, -4.0, 4.0, (BATCH, SEQ, D), jnp.float32)
    boost = 4.0
    shard_count = SEQ // TOK_DEV
    block_width = D // shard_count
    pairing = jax.random.permutation(pair_key, shard_count)
    position = jnp.arange(SEQ)
    shard_of = position // TOK_DEV
    feature_block = jnp.arange(D) // block_width
    paired = pairing[shard_of][:, None] == feature_block[None, :]
    spike = jnp.where(paired, boost, 1.0)
    ramp = 0.5 + position.astype(jnp.float32) / SEQ
    spots = jax.random.randint(spot_key, (BATCH, 4), 0, SEQ)
    struck = jnp.any(position[None, :, None] == spots[:, None, :], axis=2)
    factor = jnp.where(struck[:, :, None], 6.0 * jnp.where(paired, 1.0, 1.0)[None], ramp[None, :, None] * spike[None])
    return (base * factor).astype(jnp.bfloat16)


def draw_step_bias(key, part):
    key = jax.random.fold_in(key, 5)
    fraction = jax.random.uniform(key, (H,), jnp.float32)
    lowest = 0.01 / SEQ
    highest = 0.004
    step = jnp.exp(jnp.log(lowest) + fraction * (jnp.log(highest) - jnp.log(lowest)))
    return jnp.log(jnp.expm1(step))


def draw_decay_rate(key, part):
    key = jax.random.fold_in(key, 7)
    fraction = jax.random.uniform(key, (H,), jnp.float32)
    return jnp.exp(fraction * jnp.log(8.0))


def steps_of(key, extent, cuts, low, top_value):
    def one(dim, shards_of):
        steps = jax.random.uniform(jax.random.fold_in(jax.random.fold_in(key, 6), dim), (shards_of,), jnp.float32, low / len(cuts), top_value / len(cuts))
        return jnp.repeat(jnp.exp(steps), extent[dim] // shards_of).reshape((-1,) + (1,) * (len(extent) - dim - 1))

    gain = one(*cuts[0])
    for cut in cuts[1:]:
        gain = gain * one(*cut)
    return gain


def noise(rng, dims, spread, reach, cuts=(), kind=jnp.bfloat16):
    drawn = jax.random.normal(rng, dims, jnp.float32) * spread
    if len(cuts) > 0:
        drawn = steps_of(rng, dims, cuts, -0.22, 0.18) * drawn
    return jnp.clip(drawn, min=-reach, max=reach).astype(kind)


def setup_inputs(seed: int = 0) -> dict:
    arg_keys = jax.random.split(jax.random.key(seed), 10)
    return {
        "layer_input": draw_layer_input(jax.random.fold_in(arg_keys[9], 71), 0),
        "w_step": noise(arg_keys[1], (D, H), D ** -0.5, 0.09375, ((0, 8), (1, 2))),
        "step_bias": draw_step_bias(jax.random.fold_in(arg_keys[9], 71), 0),
        "decay_rate": draw_decay_rate(jax.random.fold_in(arg_keys[9], 71), 0),
        "ssm_input": noise(arg_keys[4], (BATCH, SEQ, H * P_SIZE), 1.0, 6.0, ((0, 8), (1, 16), (2, 2))),
        "b_input": noise(arg_keys[5], (BATCH, SEQ, G * N), 1.0, 6.0, ((0, 8), (1, 16), (2, 2))),
        "c_input": noise(arg_keys[6], (BATCH, SEQ, G * N), (N * Q) ** -0.5, 0.046875, ((0, 8), (1, 16), (2, 2))),
        "skip_gain": jnp.clip(1.0 + 0.1 * jax.random.normal(arg_keys[7], (H,), jnp.float32), 0.5, 1.5),
        "grad_y": noise(arg_keys[8], (BATCH, SEQ, H * P_SIZE), 1.0, 6.0, ((0, 8), (1, 16), (2, 2))),
    }


PRECISE = lax.Precision.HIGHEST


def block_terms(x_block, b_block, c_block, gate_block):
    length = x_block.shape[0]
    head_count = x_block.shape[1]
    groups = b_block.shape[1]
    per_group = head_count // groups
    running = jnp.cumsum(gate_block, axis=0)
    closing = running[-1]
    position = jnp.arange(length)
    causal = position[:, None] >= position[None, :]
    column = running.T
    decays = jnp.exp(jnp.where(causal[None], column[:, :, None] - column[:, None, :], -1e30))
    inner_prod = jnp.einsum("tgn,sgn->gts", c_block.astype(jnp.float32), b_block.astype(jnp.float32), precision=PRECISE)
    weighted = decays * jnp.repeat(inner_prod, per_group, axis=0)
    mixing = weighted.astype(jnp.bfloat16)
    weight = jnp.exp(closing[None, :] - running)
    scaled = (x_block.astype(jnp.float32) * weight[:, :, None]).astype(jnp.bfloat16)
    b_heads = jnp.repeat(b_block, per_group, axis=1).astype(jnp.float32)
    c_heads = jnp.repeat(c_block, per_group, axis=1).astype(jnp.float32)
    pieces = jnp.einsum("shp,shn->hpn", scaled.astype(jnp.float32), b_heads, precision=PRECISE)
    return running, closing, decays, weighted, mixing, weight, scaled, b_heads, c_heads, pieces


def forward_block(carry_state, x_block, b_block, c_block, gate_block, skip_gain):
    running, closing, decays, weighted, mixing, weight, scaled, b_heads, c_heads, pieces = block_terms(x_block, b_block, c_block, gate_block)
    x_float = x_block.astype(jnp.float32)
    direct = jnp.einsum("hts,shp->thp", mixing.astype(jnp.float32), x_float, precision=PRECISE)
    across = jnp.einsum("thn,hpn->thp", c_heads, carry_state, precision=PRECISE)
    output = (direct + jnp.exp(running)[:, :, None] * across + skip_gain[None, :, None] * x_float).astype(jnp.bfloat16)
    advanced = jnp.exp(closing)[:, None, None] * carry_state + pieces
    return advanced, output


def backward_block(back_state, carry_state, x_block, b_block, c_block, gate_block, grad_block, skip_gain):
    running, closing, decays, weighted, mixing, weight, scaled, b_heads, c_heads, pieces = block_terms(x_block, b_block, c_block, gate_block)
    length = x_block.shape[0]
    head_count = x_block.shape[1]
    groups = b_block.shape[1]
    states = b_block.shape[2]
    per_group = head_count // groups
    x_float = x_block.astype(jnp.float32)
    dy_float = grad_block.astype(jnp.float32)
    scaled_dy = dy_float * jnp.exp(running)[:, :, None]
    jump_terms = jnp.einsum("thp,thn->hpn", scaled_dy, c_heads, precision=PRECISE)
    back_proj = jnp.einsum("shn,hpn->shp", b_heads, back_state, precision=PRECISE)
    grad_x = (jnp.einsum("hts,thp->shp", mixing.astype(jnp.float32), dy_float, precision=PRECISE)
              + weight[:, :, None] * back_proj + skip_gain[None, :, None] * dy_float).astype(jnp.bfloat16)
    agreement = jnp.einsum("thp,shp->hts", dy_float, x_float, precision=PRECISE)
    grad_inner = (agreement * decays).reshape(groups, per_group, length, length).sum(axis=1).astype(jnp.bfloat16)
    across = jnp.einsum("thn,hpn->thp", c_heads, carry_state, precision=PRECISE)
    grad_c = jnp.einsum("gts,sgn->tgn", grad_inner.astype(jnp.float32), b_block.astype(jnp.float32), precision=PRECISE)
    grad_c = grad_c + jnp.einsum("thp,hpn->thn", scaled_dy, carry_state, precision=PRECISE).reshape(length, groups, per_group, states).sum(axis=2)
    grad_b = jnp.einsum("gts,tgn->sgn", grad_inner.astype(jnp.float32), c_block.astype(jnp.float32), precision=PRECISE)
    grad_b = grad_b + jnp.einsum("shp,hpn->shn", scaled.astype(jnp.float32), back_state, precision=PRECISE).reshape(length, groups, per_group, states).sum(axis=2)
    products = agreement * weighted
    state_term = weight * jnp.sum(x_float * back_proj, axis=2)
    grad_running = (products.sum(axis=2) - products.sum(axis=1)).T + jnp.sum(scaled_dy * across, axis=2) - state_term
    closing_sum = state_term.sum(axis=0) + jnp.exp(closing) * jnp.sum(carry_state * back_state, axis=(1, 2))
    position = jnp.arange(length)
    grad_running = grad_running + jnp.where(position[:, None] == length - 1, closing_sum[None, :], 0.0)
    grad_gate = jnp.cumsum(grad_running[::-1], axis=0)[::-1]
    earlier = jump_terms + jnp.exp(closing)[:, None, None] * back_state
    return earlier, (grad_x, grad_b.astype(jnp.bfloat16), grad_c.astype(jnp.bfloat16), grad_gate)


def reference(layer_input, w_step, step_bias, decay_rate, ssm_input, b_input, c_input, skip_gain, grad_y):
    sequences = layer_input.shape[0]
    length_all = layer_input.shape[1]
    features = layer_input.shape[2]
    flattened = layer_input.reshape(sequences * length_all, features)
    step_raw = jnp.dot(flattened, w_step, preferred_element_type=jnp.float32) + step_bias[None, :]
    log_gate = -decay_rate[None, :] * jax.nn.softplus(step_raw)
    block_count = length_all // Q

    def to_blocks(array, tail_shape):
        return jnp.moveaxis(array.reshape((sequences, block_count, Q) + tail_shape), 1, 0)

    def from_blocks(array):
        return jnp.moveaxis(array, 0, 1).reshape(sequences, length_all, -1)

    x_all = to_blocks(ssm_input, (H, P_SIZE))
    b_all = to_blocks(b_input, (G, N))
    c_all = to_blocks(c_input, (G, N))
    gate_all = to_blocks(log_gate.reshape(sequences, length_all, H), (H,))
    dy_all = to_blocks(grad_y, (H, P_SIZE))
    forward_many = jax.vmap(forward_block, in_axes=(0, 0, 0, 0, 0, None))
    backward_many = jax.vmap(backward_block, in_axes=(0, 0, 0, 0, 0, 0, 0, None))

    def forward_step(carry_state, inputs):
        x_block, b_block, c_block, gate_block = inputs
        advanced, output = forward_many(carry_state, x_block, b_block, c_block, gate_block, skip_gain)
        return advanced, (output, carry_state)

    zero_state = jnp.zeros((sequences, H, P_SIZE, N), jnp.float32)
    unused, (outputs, carries) = lax.scan(forward_step, zero_state, (x_all, b_all, c_all, gate_all))

    def backward_step(back_state, inputs):
        carry_state, x_block, b_block, c_block, gate_block, grad_block = inputs
        return backward_many(back_state, carry_state, x_block, b_block, c_block, gate_block, grad_block, skip_gain)

    unused_back, (grad_x, grad_b, grad_c, grad_gate) = lax.scan(
        backward_step, zero_state, (carries, x_all, b_all, c_all, gate_all, dy_all), reverse=True)
    grad_raw = (from_blocks(grad_gate).reshape(sequences * length_all, H) * (-decay_rate[None, :])
                * jax.nn.sigmoid(step_raw)).astype(jnp.bfloat16)
    grad_input = jnp.dot(grad_raw, w_step.T, preferred_element_type=jnp.float32).astype(jnp.bfloat16)
    grad_w_step = jnp.dot(flattened.T, grad_raw, preferred_element_type=jnp.float32)
    return (from_blocks(outputs), from_blocks(grad_x), from_blocks(grad_b), from_blocks(grad_c),
            grad_input.reshape(sequences, length_all, features), grad_w_step)
```

```python
import functools

import jax
import jax.numpy as jnp
from jax import lax
from jax.experimental import pallas as pl
from jax.experimental.pallas import tpu as pltpu
from jax.sharding import PartitionSpec as P

BF = jnp.bfloat16
F32 = jnp.float32
P_SIZE = 64
N = 128
Q = 128
PER_GROUP = 16
GROUPS = 4
HEADS = GROUPS * PER_GROUP
GW = PER_GROUP * P_SIZE
ROWS = 2 * N + 16
VMEM = 56 * 1024 * 1024


def dot(a, b):
    return jnp.dot(a, b, preferred_element_type=F32)


def dot_nt(a, b):
    return lax.dot_general(a, b, (((1,), (1,)), ((), ())), preferred_element_type=F32)


def dot_tn(a, b):
    return lax.dot_general(a, b, (((0,), (0,)), ((), ())), preferred_element_type=F32)


def split2(v):
    hi = v.astype(BF)
    return hi, (v - hi.astype(F32)).astype(BF)


def split3(v):
    hi = v.astype(BF)
    rest = v - hi.astype(F32)
    mid = rest.astype(BF)
    return hi, mid, (rest - mid.astype(F32)).astype(BF)


def iota(shape, dim):
    return lax.broadcasted_iota(jnp.int32, shape, dim)


def expander():
    return (iota((PER_GROUP, GW), 1) // P_SIZE == iota((PER_GROUP, GW), 0)).astype(F32).astype(BF)


def expand(v, e):
    hi, lo = split2(v)
    return dot(hi, e) + dot(lo, e)


def tri(lower):
    row, col = iota((Q, Q), 0), iota((Q, Q), 1)
    keep = row >= col if lower else row <= col
    return keep.astype(F32).astype(BF)


def scan_dot(t, v):
    a, b, c = split3(v)
    return dot(t, a) + dot(t, b) + dot(t, c)


def softplus(v):
    return jnp.maximum(v, 0.0) + jnp.log1p(jnp.exp(-jnp.abs(v)))


def pieces_kernel(
    idx, li_own, li_oth, w, bias, rate, x, dy, b, c, s0, s1, s2, s3, step_o, run_o, runt_o
):
    half = li_own.shape[1]
    me, z = idx[0], idx[1]
    own = pl.multiple_of(me * half, half)
    oth = pl.multiple_of((1 - me) * half, half)
    step = (
        dot(li_own[...], w[pl.ds(own, half), :])
        + dot(li_oth[...], w[pl.ds(oth, half), :])
        + bias[...]
    )
    step_o[...] = step
    running = scan_dot(tri(True), -rate[...] * softplus(step))
    runt_o[...] = jnp.swapaxes(running, 0, 1)
    for g in range(GROUPS):
        run_o[g] = running[:, g * PER_GROUP : (g + 1) * PER_GROUP]
    e = expander()
    for s, out in enumerate((s0, s1, s2, s3)):
        g = lax.rem(z + s, GROUPS)
        run = run_o[g]
        closing = run[Q - 1 :, :]
        weight = expand(jnp.exp(closing - run), e)
        early = expand(jnp.exp(run), e)
        wide = pl.ds(pl.multiple_of(g * GW, GW), GW)
        slim = pl.ds(pl.multiple_of(g * N, N), N)
        scaled = (x[:, wide].astype(F32) * weight).astype(BF)
        scaled_dy = (dy[:, wide].astype(F32) * early).astype(BF)
        out[:N, :] = dot_tn(b[:, slim], scaled).astype(BF)
        out[N : 2 * N, :] = dot_tn(c[:, slim], scaled_dy).astype(BF)
        last = early[Q - 1 :, :]
        rest = last - last.astype(BF).astype(F32)
        out[2 * N :, :] = jnp.where(iota((16, GW), 0) < 8, last, rest).astype(BF)


def local_kernel(x, dy, b, c, run, runt, direct_o, gdirect_o, gc_o, gb_o):
    bg, cg = b[...], c[...]
    inner = dot_nt(cg, bg)
    inner2 = jnp.concatenate([inner, inner], axis=1)
    row, col = iota((Q, 2 * Q), 0), iota((Q, 2 * Q), 1)
    causal = row >= lax.rem(col, Q)
    first = iota((Q, 2 * P_SIZE), 1) < P_SIZE
    m1 = first.astype(F32).astype(BF)
    m2 = 1 - m1
    total = jnp.zeros((Q, Q), F32)
    for j in range(PER_GROUP // 2):
        lanes = slice(j * 2 * P_SIZE, (j + 1) * 2 * P_SIZE)
        xp, dyp = x[:, lanes], dy[:, lanes]
        xbd = jnp.concatenate([xp * m1, xp * m2], axis=0)
        diff = jnp.concatenate(
            [
                run[0, :, 2 * j + i : 2 * j + i + 1] - runt[2 * j + i : 2 * j + i + 1, :]
                for i in range(2)
            ],
            axis=1,
        )
        dec = jnp.exp(jnp.where(causal, diff, -1e30))
        ad = dot_nt(dyp, xbd) * dec
        total = total + ad[:, :Q] + ad[:, Q:]
        mix = (dec * inner2).astype(BF)
        direct_o[:, lanes] = dot(mix, xbd)
        both = dot_tn(mix, dyp)
        gdirect_o[:, lanes] = jnp.where(first, both[:Q], both[Q:])
    grad_inner = total.astype(BF)
    gc_o[...] = dot(grad_inner, bg)
    gb_o[...] = dot_tn(grad_inner, cg)


def decay_of(msg):
    tail = msg[2 * N :, :].astype(F32)
    return tail[0:1, :] + tail[8:9, :]


def row_kernel(idx, r0, r1, r2, r3, fwd_o, bwd_o, ordered):
    z = idx[1]
    for s, r in enumerate((r0, r1, r2, r3)):
        ordered[lax.rem(z - s + GROUPS, GROUPS)] = r[...]
    decays = [decay_of(ordered.at[k]) for k in range(GROUPS)]
    total = ordered[0, :N, :].astype(F32)
    for k in range(1, GROUPS):
        total = decays[k] * total + ordered[k, :N, :].astype(F32)
    back = ordered[GROUPS - 1, N : 2 * N, :].astype(F32)
    for k in range(GROUPS - 2, -1, -1):
        back = decays[k] * back + ordered[k, N : 2 * N, :].astype(F32)
    decay = decays[0]
    for k in range(1, GROUPS):
        decay = decay * decays[k]
    rest = decay - decay.astype(BF).astype(F32)
    tail = jnp.where(iota((16, GW), 0) < 8, decay, rest).astype(BF)
    fwd_o[:N, :] = total.astype(BF)
    fwd_o[N:, :] = tail
    bwd_o[:N, :] = back.astype(BF)
    bwd_o[N:, :] = tail


def carry_kernel(count, *refs):
    idx, r0, r1, r2, r3 = refs[:5]
    fwd = refs[5 : 5 + count]
    bwd = refs[5 + count : 5 + 2 * count]
    outs = refs[5 + 2 * count : 9 + 2 * count]
    ordered, carries = refs[9 + 2 * count :]
    z = idx[1]
    for s, r in enumerate((r0, r1, r2, r3)):
        ordered[lax.rem(z - s + GROUPS, GROUPS)] = r[...]

    def entering(parts):
        value = jnp.zeros((N, GW), F32)
        for part in parts[::-1]:
            tail = part[N:, :].astype(F32)
            value = (tail[0:1, :] + tail[8:9, :]) * value + part[:N, :].astype(F32)
        return value

    decays = [decay_of(ordered.at[k]) for k in range(GROUPS)]
    value = entering(fwd)
    for k in range(GROUPS):
        carries[k, :N, :] = value.astype(BF)
        if k < GROUPS - 1:
            value = decays[k] * value + ordered[k, :N, :].astype(F32)
    value = entering(bwd)
    for k in range(GROUPS - 1, -1, -1):
        carries[k, N:, :] = value.astype(BF)
        if k > 0:
            value = decays[k] * value + ordered[k, N : 2 * N, :].astype(F32)
    for s, out in enumerate(outs):
        out[...] = carries[lax.rem(z + s, GROUPS)]


def finish_kernel(
    idx,
    c0,
    c1,
    c2,
    c3,
    x,
    dy,
    b,
    c,
    run_i,
    step,
    rate,
    skip,
    direct,
    gdirect,
    gc_i,
    gb_i,
    out_o,
    gx_o,
    gb_o,
    gc_o,
    raw_o,
    gr,
):
    z = idx[1]
    e = expander()
    for s, msg in enumerate((c0, c1, c2, c3)):
        g = lax.rem(z - s + GROUPS, GROUPS)
        run = run_i[g]
        weight = expand(jnp.exp(run[Q - 1 :, :] - run), e)
        early = expand(jnp.exp(run), e)
        gain = expand(jnp.broadcast_to(skip[g], (8, PER_GROUP)), e)[0:1, :]
        wide = pl.ds(pl.multiple_of(g * GW, GW), GW)
        slim = pl.ds(pl.multiple_of(g * N, N), N)
        carry, back = msg[:N, :], msg[N:, :]
        xg, dyg = x[:, wide].astype(F32), dy[:, wide].astype(F32)
        y = direct[:, wide] + early * dot(c[:, slim], carry)
        out_o[:, wide] = (y + gain * xg).astype(BF)
        lateral = weight * dot(b[:, slim], back)
        gx = gdirect[:, wide] + lateral
        gx_o[:, wide] = (gx + gain * dyg).astype(BF)
        gc_o[:, slim] = (gc_i[:, slim] + dot_nt((dyg * early).astype(BF), carry)).astype(BF)
        gb_o[:, slim] = (gb_i[:, slim] + dot_nt((xg * weight).astype(BF), back)).astype(BF)
        closing = jnp.sum(xg * lateral, axis=0, keepdims=True) + early[Q - 1 :, :] * jnp.sum(
            carry.astype(F32) * back.astype(F32), axis=0, keepdims=True
        )
        terms = dyg * y - xg * gx + jnp.where(iota((Q, GW), 0) == Q - 1, closing, 0.0)
        hi, lo = split2(terms)
        gr[g] = dot_nt(hi, e) + dot_nt(lo, e)
    grad_running = jnp.concatenate([gr[g] for g in range(GROUPS)], axis=1)
    gate = scan_dot(tri(False), grad_running)
    raw_o[...] = (gate * -rate[...] * jax.nn.sigmoid(step[...])).astype(BF)


def project_kernel(idx, li_own, li_oth, raw, part_o):
    half = li_own.shape[1]
    width = part_o.shape[2]
    per = half // width
    r = raw[...]
    for source, base in ((li_own, idx[0] * per), (li_oth, (1 - idx[0]) * per)):
        whole = dot_tn(r, source[...]).astype(BF)
        for k in range(per):
            part_o[base + k] = whole[:, k * width : (k + 1) * width]


def input_kernel(idx, raw, raw_oth, w, w_oth, out):
    half = w_oth.shape[0]
    own = pl.multiple_of(idx[0] * half, half)
    out[...] = (
        dot_nt(raw[...], w[pl.ds(own, half), :]) + dot_nt(raw_oth[...], w_oth[...])
    ).astype(BF)


def replicas_kernel(parts, out):
    count, _, lanes = out.shape
    total = parts[0].astype(F32)
    for k in range(1, parts.shape[0]):
        total = total + parts[k].astype(F32)
    across = total.shape[1] // lanes
    for k in range(count):
        i, j = k // across, k % across
        out[k] = total[i * 8 : (i + 1) * 8, j * lanes : (j + 1) * lanes]


def shares_kernel(parts, out):
    total = parts[0]
    for k in range(1, parts.shape[0]):
        total = total + parts[k]
    for k in range(out.shape[0]):
        out[k] = total


def weights_kernel(parts, out):
    count, _, lanes = parts.shape
    across = out.shape[0] // lanes
    rows = [
        jnp.concatenate([parts[i * across + j] for j in range(across)], axis=1)
        for i in range(count // across)
    ]
    out[...] = jnp.swapaxes(jnp.concatenate(rows, axis=0), 0, 1)


SMEM_SPEC = pl.BlockSpec(memory_space=pltpu.SMEM)
VMEM_SPEC = pl.BlockSpec(memory_space=pltpu.VMEM)


def sds(shape, dtype):
    return jax.ShapeDtypeStruct(shape, dtype)


def call(kernel, name, outs, *args, scratch=(), scalars=1, cost=0):
    params = pltpu.CompilerParams(vmem_limit_bytes=VMEM)
    return pl.pallas_call(
        kernel,
        out_shape=outs,
        in_specs=[SMEM_SPEC] * scalars + [VMEM_SPEC] * (len(args) - scalars),
        out_specs=jax.tree.map(lambda _: VMEM_SPEC, outs),
        scratch_shapes=list(scratch),
        compiler_params=params,
        name=name,
    )(*args)


def shards(
    layer_input, w_step, step_bias, decay_rate, ssm_input, b_input, c_input, skip_gain, grad_y
):
    dp, ctx = lax.axis_size("dp"), lax.axis_size("ctx")
    nz = GROUPS
    ny = ctx // nz
    me = lax.axis_index("head")
    z = lax.rem(lax.axis_index("ctx"), nz)
    idx = jnp.stack([me, z]).astype(jnp.int32)
    swap = [(0, 1), (1, 0)]

    def z_shift(v, s):
        pairs = [(y * nz + k, y * nz + (k + s) % nz) for y in range(ny) for k in range(nz)]
        return lax.ppermute(v, "ctx", pairs)

    def y_shift(v, s):
        pairs = [(y * nz + k, (y + s) * nz + k) for y in range(ny) if 0 <= y + s < ny for k in range(nz)]
        return lax.ppermute(v, "ctx", pairs)

    li = layer_input[0]
    x, dy, b, c = ssm_input[0], grad_y[0], b_input[0], c_input[0]
    half = li.shape[1]
    bias, rate = step_bias.reshape(1, HEADS), decay_rate.reshape(1, HEADS)
    skip = skip_gain.reshape(GROUPS, 1, PER_GROUP)

    li_oth = lax.ppermute(li, "head", swap)
    w = lax.all_gather(w_step, "dp", axis=0, tiled=True)
    w_oth = lax.ppermute(lax.dynamic_slice_in_dim(w, (1 - me) * half, half, 0), "head", swap)

    *sent, step, run, runt = call(
        pieces_kernel,
        "pieces",
        [sds((ROWS, GW), BF)] * GROUPS
        + [sds((Q, HEADS), F32), sds((GROUPS, Q, PER_GROUP), F32), sds((HEADS, Q), F32)],
        idx, li, li_oth, w, bias, rate, x, dy, b, c,
    )
    got = [sent[0]] + [z_shift(sent[s], s) for s in range(1, nz)]

    direct, gdirect, gc, gb = pl.pallas_call(
        local_kernel,
        grid=(GROUPS,),
        out_shape=[
            sds((Q, GROUPS * GW), F32),
            sds((Q, GROUPS * GW), F32),
            sds((Q, GROUPS * N), F32),
            sds((Q, GROUPS * N), F32),
        ],
        in_specs=[
            pl.BlockSpec((Q, GW), lambda g: (0, g)),
            pl.BlockSpec((Q, GW), lambda g: (0, g)),
            pl.BlockSpec((Q, N), lambda g: (0, g)),
            pl.BlockSpec((Q, N), lambda g: (0, g)),
            pl.BlockSpec((1, Q, PER_GROUP), lambda g: (g, 0, 0)),
            pl.BlockSpec((PER_GROUP, Q), lambda g: (g, 0)),
        ],
        out_specs=[
            pl.BlockSpec((Q, GW), lambda g: (0, g)),
            pl.BlockSpec((Q, GW), lambda g: (0, g)),
            pl.BlockSpec((Q, N), lambda g: (0, g)),
            pl.BlockSpec((Q, N), lambda g: (0, g)),
        ],
        compiler_params=pltpu.CompilerParams(vmem_limit_bytes=VMEM),
        cost_estimate=pl.CostEstimate(
            flops=4_000_000_000, bytes_accessed=12_000_000, transcendentals=1_100_000
        ),
        name="local",
    )(x, dy, b, c, run, runt)

    ordered = pltpu.VMEM((GROUPS, ROWS, GW), BF)
    fwd, bwd = call(
        row_kernel, "row", [sds((N + 16, GW), BF)] * 2, idx, *got, scratch=[ordered]
    )
    fwds = [y_shift(fwd, s) for s in range(1, ny)]
    bwds = [y_shift(bwd, -s) for s in range(1, ny)]
    back_sent = call(
        functools.partial(carry_kernel, ny - 1),
        "carry",
        [sds((2 * N, GW), BF)] * GROUPS,
        idx, *got, *fwds, *bwds,
        scratch=[ordered, pltpu.VMEM((GROUPS, 2 * N, GW), BF)],
    )
    states = [back_sent[0]] + [z_shift(back_sent[s], s) for s in range(1, nz)]

    output, grad_x, grad_b, grad_c, raw = call(
        finish_kernel,
        "finish",
        [
            sds((Q, GROUPS * GW), BF),
            sds((Q, GROUPS * GW), BF),
            sds((Q, GROUPS * N), BF),
            sds((Q, GROUPS * N), BF),
            sds((Q, HEADS), BF),
        ],
        idx, *states, x, dy, b, c, run, step, rate, skip, direct, gdirect, gc, gb,
        scratch=[pltpu.VMEM((GROUPS, Q, PER_GROUP), F32)],
    )
    raw_oth = lax.ppermute(raw, "head", swap)

    rows = 2 * half // dp
    lanes = HEADS * rows // (8 * ctx)
    part = call(project_kernel, "project", sds((dp, HEADS, rows), BF), idx, li, li_oth, raw)
    part = lax.all_to_all(part, "dp", 0, 0, tiled=True)
    share = call(replicas_kernel, "replicas", sds((ctx, 8, lanes), F32), part, scalars=0)
    share = lax.all_to_all(share, "ctx", 0, 0, tiled=True)
    share = call(shares_kernel, "shares", sds((ctx, 8, lanes), F32), share, scalars=0)
    share = lax.all_to_all(share, "ctx", 0, 0, tiled=True)
    grad_w = call(weights_kernel, "weights", sds((rows, HEADS), F32), share, scalars=0)

    grad_input = call(input_kernel, "input", sds((Q, half), BF), idx, raw, raw_oth, w, w_oth)
    return output[None], grad_x[None], grad_b[None], grad_c[None], grad_input[None], grad_w


def solution(mesh):
    tokens = P("dp", "ctx", "head")
    in_specs = (
        tokens, P("dp", "head"), P("head"), P("head"), tokens, tokens, tokens, P("head"), tokens,
    )
    out_specs = (tokens, tokens, tokens, tokens, tokens, P("dp", "head"))
    return jax.shard_map(shards, mesh=mesh, in_specs=in_specs, out_specs=out_specs, check_vma=False)
```

```python
import functools

import jax
import jax.numpy as jnp
from jax import lax
from jax.experimental import pallas as pl
from jax.experimental.pallas import tpu as pltpu
from jax.sharding import PartitionSpec as P

BF = jnp.bfloat16
F32 = jnp.float32
P_SIZE = 64
N = 128
Q = 128
PER_GROUP = 16
GROUPS = 4
HEADS = GROUPS * PER_GROUP
GW = PER_GROUP * P_SIZE
ROWS = 2 * N + 16
PARTS = 2
PG = GROUPS // PARTS
VMEM = 56 * 1024 * 1024


def dot(a, b):
    return jnp.dot(a, b, preferred_element_type=F32)


def dot_nt(a, b):
    return lax.dot_general(a, b, (((1,), (1,)), ((), ())), preferred_element_type=F32)


def dot_tn(a, b):
    return lax.dot_general(a, b, (((0,), (0,)), ((), ())), preferred_element_type=F32)


def split2(v):
    hi = v.astype(BF)
    return hi, (v - hi.astype(F32)).astype(BF)


def split3(v):
    hi = v.astype(BF)
    rest = v - hi.astype(F32)
    mid = rest.astype(BF)
    return hi, mid, (rest - mid.astype(F32)).astype(BF)


def iota(shape, dim):
    return lax.broadcasted_iota(jnp.int32, shape, dim)


def expander():
    return (iota((PER_GROUP, GW), 1) // P_SIZE == iota((PER_GROUP, GW), 0)).astype(F32).astype(BF)


def expand(v, e):
    hi, lo = split2(v)
    return dot(hi, e) + dot(lo, e)


def tri(lower):
    row, col = iota((Q, Q), 0), iota((Q, Q), 1)
    keep = row >= col if lower else row <= col
    return keep.astype(F32).astype(BF)


def scan_dot(t, v):
    a, b, c = split3(v)
    return dot(t, a) + dot(t, b) + dot(t, c)


def softplus(v):
    return jnp.maximum(v, 0.0) + jnp.log1p(jnp.exp(-jnp.abs(v)))


def gates_kernel(idx, li_own, li_oth, w, bias, rate, step_o, run_o, runt_o):
    count, _, rows = w.shape
    per = count // 2
    step = bias[...]
    for k in range(per):
        cols = slice(k * rows, (k + 1) * rows)
        step = step + dot_nt(li_own[:, cols], w[idx[0] * per + k])
        step = step + dot_nt(li_oth[:, cols], w[(1 - idx[0]) * per + k])
    step_o[...] = step
    running = scan_dot(tri(True), -rate[...] * softplus(step))
    runt_o[...] = jnp.swapaxes(running, 0, 1)
    for g in range(GROUPS):
        run_o[g] = running[:, g * PER_GROUP : (g + 1) * PER_GROUP]


def pieces_kernel(x, dy, b, c, run, out):
    e = expander()
    r = run[0]
    weight = expand(jnp.exp(r[Q - 1 :, :] - r), e)
    early = expand(jnp.exp(r), e)
    scaled = (x[...].astype(F32) * weight).astype(BF)
    scaled_dy = (dy[...].astype(F32) * early).astype(BF)
    piece = dot_tn(b[...], scaled).astype(BF)
    jump = dot_tn(c[...], scaled_dy).astype(BF)
    last = early[Q - 1 :, :]
    rest = last - last.astype(BF).astype(F32)
    tail = jnp.where(iota((16, GW), 0) < 8, last, rest).astype(BF)
    shares, _, width = out.shape
    for k in range(shares):
        lanes = slice(k * width, (k + 1) * width)
        out[k, :N, :] = piece[:, lanes]
        out[k, N : 2 * N, :] = jump[:, lanes]
        out[k, 2 * N :, :] = tail[:, lanes]


def local_kernel(x, dy, b, c, run, runt, direct_o, gdirect_o, gc_o, gb_o):
    bg, cg = b[...], c[...]
    inner = dot_nt(cg, bg)
    inner2 = jnp.concatenate([inner, inner], axis=1)
    row, col = iota((Q, 2 * Q), 0), iota((Q, 2 * Q), 1)
    causal = row >= lax.rem(col, Q)
    first = iota((Q, 2 * P_SIZE), 1) < P_SIZE
    m1 = first.astype(F32).astype(BF)
    m2 = 1 - m1
    total = jnp.zeros((Q, Q), F32)
    for j in range(PER_GROUP // 2):
        lanes = slice(j * 2 * P_SIZE, (j + 1) * 2 * P_SIZE)
        xp, dyp = x[:, lanes], dy[:, lanes]
        xbd = jnp.concatenate([xp * m1, xp * m2], axis=0)
        diff = jnp.concatenate(
            [
                run[0, :, 2 * j + i : 2 * j + i + 1] - runt[2 * j + i : 2 * j + i + 1, :]
                for i in range(2)
            ],
            axis=1,
        )
        dec = jnp.exp(jnp.where(causal, diff, -1e30))
        ad = dot_nt(dyp, xbd) * dec
        total = total + ad[:, :Q] + ad[:, Q:]
        mix = (dec * inner2).astype(BF)
        direct_o[:, lanes] = dot(mix, xbd)
        both = dot_tn(mix, dyp)
        gdirect_o[:, lanes] = jnp.where(first, both[:Q], both[Q:])
    grad_inner = total.astype(BF)
    gc_o[...] = dot(grad_inner, bg)
    gb_o[...] = dot_tn(grad_inner, cg)


def scan_kernel(msgs, out):
    count, _, width = msgs.shape

    def decay(k):
        tail = msgs[k, 2 * N :, :].astype(F32)
        return tail[0:1, :] + tail[8:9, :]

    carry = jnp.zeros((N, width), F32)
    for k in range(count):
        out[k, :N, :] = carry.astype(BF)
        if k < count - 1:
            carry = decay(k) * carry + msgs[k, :N, :].astype(F32)
    back = jnp.zeros((N, width), F32)
    for k in range(count - 1, -1, -1):
        out[k, N:, :] = back.astype(BF)
        if k > 0:
            back = decay(k) * back + msgs[k, N : 2 * N, :].astype(F32)


def finish_kernel(part, *refs):
    states, x, dy, b, c, run, skip, direct, gdirect, gc_i, gb_i = refs[:11]
    out_o, gx_o, gb_o, gc_o, gr_o = refs[-5:]
    e = expander()
    r = run[0]
    weight = expand(jnp.exp(r[Q - 1 :, :] - r), e)
    early = expand(jnp.exp(r), e)
    gain = expand(jnp.broadcast_to(skip[0], (8, PER_GROUP)), e)[0:1, :]
    carry = jnp.concatenate([states[k, :N, :] for k in range(states.shape[0])], axis=1)
    back = jnp.concatenate([states[k, N:, :] for k in range(states.shape[0])], axis=1)
    xg, dyg = x[...].astype(F32), dy[...].astype(F32)
    y = direct[...] + early * dot(c[...], carry)
    out_o[...] = (y + gain * xg).astype(BF)
    lateral = weight * dot(b[...], back)
    gx = gdirect[...] + lateral
    gx_o[...] = (gx + gain * dyg).astype(BF)
    gc_o[...] = (gc_i[...] + dot_nt((dyg * early).astype(BF), carry)).astype(BF)
    gb_o[...] = (gb_i[...] + dot_nt((xg * weight).astype(BF), back)).astype(BF)
    closing = jnp.sum(xg * lateral, axis=0, keepdims=True) + early[Q - 1 :, :] * jnp.sum(
        carry.astype(F32) * back.astype(F32), axis=0, keepdims=True
    )
    terms = dyg * y - xg * gx + jnp.where(iota((Q, GW), 0) == Q - 1, closing, 0.0)
    hi, lo = split2(terms)
    gr_o[0] = dot_nt(hi, e) + dot_nt(lo, e)


def raw_kernel(step, rate, *refs):
    raw_o, rawt_o = refs[-2:]
    grad_running = jnp.concatenate([gr[k] for gr in refs[:-2] for k in range(PG)], axis=1)
    gate = scan_dot(tri(False), grad_running)
    raw = gate * -rate[...] * jax.nn.sigmoid(step[...])
    raw_o[...] = raw.astype(BF)
    rawt = jnp.swapaxes(raw, 0, 1).astype(BF)
    for k in range(rawt_o.shape[0]):
        rawt_o[k] = rawt


def deal_kernel(idx, li_own, li_oth, *outs):
    count = len(outs)
    rows = outs[0].shape[1]
    per = count // 2
    for s, out in enumerate(outs):
        k = lax.rem(idx[1] + s, count)
        cols = pl.ds(pl.multiple_of(lax.rem(k, per) * rows, rows), rows)

        @pl.when(k // per == idx[0])
        def _():
            out[...] = li_own[:, cols]

        @pl.when(k // per != idx[0])
        def _():
            out[...] = li_oth[:, cols]


def rows_kernel(idx, rawt, *refs):
    out = refs[-1]
    count = len(refs) - 1
    total = jnp.zeros(out.shape, F32)
    for s in range(count):
        total = total + dot(rawt[lax.rem(idx[1] - s + count, count)], refs[s][...])
    out[...] = total.astype(out.dtype)


def add_kernel(*refs):
    a, b, c, d = (ref[...].astype(F32) for ref in refs[:-1])
    refs[-1][...] = ((a + c) + (b + d)).astype(refs[-1].dtype)


def input_kernel(idx, raw, raw_oth, w, w_oth, out):
    per, _, rows = w_oth.shape
    for k in range(per):
        out[:, k * rows : (k + 1) * rows] = (
            dot(raw[...], w[idx[0] * per + k]) + dot(raw_oth[...], w_oth[k])
        ).astype(BF)


SMEM_SPEC = pl.BlockSpec(memory_space=pltpu.SMEM)
VMEM_SPEC = pl.BlockSpec(memory_space=pltpu.VMEM)


def sds(shape, dtype):
    return jax.ShapeDtypeStruct(shape, dtype)


def call(kernel, name, outs, *args, scratch=(), scalars=0):
    params = pltpu.CompilerParams(vmem_limit_bytes=VMEM)
    return pl.pallas_call(
        kernel,
        out_shape=outs,
        in_specs=[SMEM_SPEC] * scalars + [VMEM_SPEC] * (len(args) - scalars),
        out_specs=jax.tree.map(lambda _: VMEM_SPEC, outs),
        scratch_shapes=list(scratch),
        compiler_params=params,
        name=name,
    )(*args)


def columns(width, first=0):
    return pl.BlockSpec((Q, width), lambda g: (0, g + first))


def heads_of(first=0):
    return pl.BlockSpec((1, Q, PER_GROUP), lambda g: (g + first, 0, 0))


def shards(
    layer_input, w_step, step_bias, decay_rate, ssm_input, b_input, c_input, skip_gain, grad_y
):
    dp, ctx = lax.axis_size("dp"), lax.axis_size("ctx")
    nz = GROUPS
    ny = ctx // nz
    me = lax.axis_index("head")
    idx = jnp.stack([me, lax.axis_index("dp")]).astype(jnp.int32)
    swap = [(0, 1), (1, 0)]
    params = pltpu.CompilerParams(vmem_limit_bytes=VMEM)

    def z_shift(v, s):
        pairs = [(y * nz + k, y * nz + (k + s) % nz) for y in range(ny) for k in range(nz)]
        return lax.ppermute(v, "ctx", pairs)

    def y_shift(v, s):
        pairs = [(y * nz + k, (y + s) % ny * nz + k) for y in range(ny) for k in range(nz)]
        return lax.ppermute(v, "ctx", pairs)

    li = layer_input[0]
    x, dy, b, c = ssm_input[0], grad_y[0], b_input[0], c_input[0]
    half = li.shape[1]
    rows = w_step.shape[0]
    per = half // rows
    bias, rate = step_bias.reshape(1, HEADS), decay_rate.reshape(1, HEADS)
    skip = skip_gain.reshape(GROUPS, 1, PER_GROUP)

    li_oth = lax.ppermute(li, "head", swap)
    w = lax.all_gather(w_step.T, "dp")
    step, run, runt = call(
        gates_kernel,
        "gates",
        [sds((Q, HEADS), F32), sds((GROUPS, Q, PER_GROUP), F32), sds((HEADS, Q), F32)],
        idx, li, li_oth, w, bias, rate,
        scalars=1,
    )

    width = PG * GW // ctx
    shares = GW // width
    sent = []
    for part in range(PARTS):
        at = part * PG
        sent.append(
            pl.pallas_call(
                pieces_kernel,
                grid=(PG,),
                out_shape=sds((ctx, ROWS, width), BF),
                in_specs=[columns(GW, at), columns(GW, at), columns(N, at), columns(N, at), heads_of(at)],
                out_specs=pl.BlockSpec((shares, ROWS, width), lambda g: (g, 0, 0)),
                compiler_params=params,
                name=f"pieces{part}",
            )(x, dy, b, c, run)
        )
    got = [lax.all_to_all(v, "ctx", 0, 0, tiled=True) for v in sent]

    w_oth = lax.ppermute(lax.dynamic_slice_in_dim(w, (1 - me) * per, per, 0), "head", swap)
    dealt = call(deal_kernel, "deal", [sds((Q, rows), BF)] * dp, idx, li, li_oth, scalars=1)
    li_rows = [dealt[0]] + [
        lax.ppermute(dealt[s], "dp", [(k, (k + s) % dp) for k in range(dp)]) for s in range(1, dp)
    ]

    direct, gdirect, gc, gb = pl.pallas_call(
        local_kernel,
        grid=(GROUPS,),
        out_shape=[
            sds((Q, GROUPS * GW), F32),
            sds((Q, GROUPS * GW), F32),
            sds((Q, GROUPS * N), F32),
            sds((Q, GROUPS * N), F32),
        ],
        in_specs=[
            columns(GW), columns(GW), columns(N), columns(N), heads_of(),
            pl.BlockSpec((PER_GROUP, Q), lambda g: (g, 0)),
        ],
        out_specs=[columns(GW), columns(GW), columns(N), columns(N)],
        compiler_params=params,
        cost_estimate=pl.CostEstimate(
            flops=4_000_000_000, bytes_accessed=12_000_000, transcendentals=1_100_000
        ),
        name="local",
    )(x, dy, b, c, run, runt)

    states = []
    for part in range(PARTS):
        back = call(scan_kernel, f"scan{part}", sds((ctx, 2 * N, width), BF), got[part])
        states.append(lax.all_to_all(back, "ctx", 0, 0, tiled=True))

    outs = []
    grads = []
    for part in range(PARTS):
        at = part * PG
        args = [states[part], x, dy, b, c, run, skip, direct, gdirect, gc, gb]
        *outs, gr = pl.pallas_call(
            functools.partial(finish_kernel, part),
            grid=(PG,),
            out_shape=[
                sds((Q, GROUPS * GW), BF),
                sds((Q, GROUPS * GW), BF),
                sds((Q, GROUPS * N), BF),
                sds((Q, GROUPS * N), BF),
                sds((PG, Q, PER_GROUP), F32),
            ],
            in_specs=[
                pl.BlockSpec((shares, 2 * N, width), lambda g: (g, 0, 0)),
                columns(GW, at), columns(GW, at), columns(N, at), columns(N, at), heads_of(at),
                pl.BlockSpec((1, 1, PER_GROUP), lambda g, at=at: (g + at, 0, 0)),
                columns(GW, at), columns(GW, at), columns(N, at), columns(N, at),
            ]
            + [pl.BlockSpec(memory_space=pl.ANY)] * len(outs),
            out_specs=[columns(GW, at), columns(GW, at), columns(N, at), columns(N, at), heads_of()],
            input_output_aliases={len(args) + k: k for k in range(len(outs))},
            compiler_params=params,
            cost_estimate=pl.CostEstimate(
                flops=1_000_000_000, bytes_accessed=6_000_000, transcendentals=100_000
            ),
            name=f"finish{part}",
        )(*args, *outs)
        grads.append(gr)
    output, grad_x, grad_b, grad_c = outs

    raw, rawt = call(
        raw_kernel, "raw", [sds((Q, HEADS), BF), sds((dp, HEADS, Q), BF)], step, rate, *grads
    )
    raw_oth = lax.ppermute(raw, "head", swap)
    rawt = lax.all_to_all(rawt, "dp", 0, 0, tiled=True)
    share = call(rows_kernel, "rows", sds((HEADS, rows), BF), idx, rawt, *li_rows, scalars=1)
    share = call(
        add_kernel, "add_z", sds((HEADS, rows), BF),
        share, *[z_shift(share, s) for s in range(1, nz)],
    )
    grad_w = call(
        add_kernel, "add_y", sds((HEADS, rows), F32),
        share, *[y_shift(share, s) for s in range(1, ny)],
    )
    grad_input = call(
        input_kernel, "input", sds((Q, half), BF), idx, raw, raw_oth, w, w_oth, scalars=1
    )
    return output[None], grad_x[None], grad_b[None], grad_c[None], grad_input[None], grad_w.T


def solution(mesh):
    tokens = P("dp", "ctx", "head")
    in_specs = (
        tokens, P("dp", "head"), P("head"), P("head"), tokens, tokens, tokens, P("head"), tokens,
    )
    out_specs = (tokens, tokens, tokens, tokens, tokens, P("dp", "head"))
    return jax.shard_map(shards, mesh=mesh, in_specs=in_specs, out_specs=out_specs, check_vma=False)
```

```python
import functools

import jax
import jax.numpy as jnp
from jax import lax
from jax.experimental import pallas as pl
from jax.experimental.pallas import tpu as pltpu
from jax.sharding import PartitionSpec as P

BF = jnp.bfloat16
F32 = jnp.float32
P_SIZE = 64
N = 128
Q = 128
PER_GROUP = 16
GROUPS = 4
HEADS = GROUPS * PER_GROUP
GW = PER_GROUP * P_SIZE
ROWS = 2 * N + 16
PARTS = 1
PG = GROUPS // PARTS
SMALL = 20 * 1024 * 1024
LARGE = 56 * 1024 * 1024


def dot(a, b):
    return jnp.dot(a, b, preferred_element_type=F32)


def dot_nt(a, b):
    return lax.dot_general(a, b, (((1,), (1,)), ((), ())), preferred_element_type=F32)


def dot_tn(a, b):
    return lax.dot_general(a, b, (((0,), (0,)), ((), ())), preferred_element_type=F32)


def split2(v):
    hi = v.astype(BF)
    return hi, (v - hi.astype(F32)).astype(BF)


def split3(v):
    hi = v.astype(BF)
    rest = v - hi.astype(F32)
    mid = rest.astype(BF)
    return hi, mid, (rest - mid.astype(F32)).astype(BF)


def iota(shape, dim):
    return lax.broadcasted_iota(jnp.int32, shape, dim)


def expander():
    return (iota((PER_GROUP, GW), 1) // P_SIZE == iota((PER_GROUP, GW), 0)).astype(F32).astype(BF)


def expand(v, e):
    return dot(jnp.concatenate(split2(v), axis=1), jnp.concatenate([e, e], axis=0))


def tri(lower):
    row, col = iota((Q, Q), 0), iota((Q, Q), 1)
    keep = row >= col if lower else row <= col
    return keep.astype(F32).astype(BF)


def scan_dot(t, v):
    a, b, c = split3(v)
    return dot(t, a) + dot(t, b) + dot(t, c)


def softplus(v):
    return jnp.maximum(v, 0.0) + jnp.log1p(jnp.exp(-jnp.abs(v)))


def gates_kernel(idx, li_own, li_oth, w, bias, rate, step_o, run_o, runt_o):
    count, _, rows = w.shape
    per = count // 2
    step = bias[...]
    for k in range(per):
        cols = slice(k * rows, (k + 1) * rows)
        step = step + dot_nt(li_own[:, cols], w[idx[0] * per + k])
        step = step + dot_nt(li_oth[:, cols], w[(1 - idx[0]) * per + k])
    step_o[...] = step
    running = scan_dot(tri(True), -rate[...] * softplus(step))
    runt_o[...] = jnp.swapaxes(running, 0, 1)
    for g in range(GROUPS):
        run_o[g] = running[:, g * PER_GROUP : (g + 1) * PER_GROUP]


def pieces_kernel(x, dy, b, c, run, out):
    e = expander()
    r = run[0]
    weight = expand(jnp.exp(r[Q - 1 :, :] - r), e)
    early = expand(jnp.exp(r), e)
    scaled = (x[...].astype(F32) * weight).astype(BF)
    scaled_dy = (dy[...].astype(F32) * early).astype(BF)
    piece = dot_tn(b[...], scaled).astype(BF)
    jump = dot_tn(c[...], scaled_dy).astype(BF)
    last = early[Q - 1 :, :]
    rest = last - last.astype(BF).astype(F32)
    tail = jnp.where(iota((16, GW), 0) < 8, last, rest).astype(BF)
    shares, _, width = out.shape
    for k in range(shares):
        lanes = slice(k * width, (k + 1) * width)
        out[k, :N, :] = piece[:, lanes]
        out[k, N : 2 * N, :] = jump[:, lanes]
        out[k, 2 * N :, :] = tail[:, lanes]


def local_kernel(x, dy, b, c, run, runt, direct_o, gdirect_o, gc_o, gb_o):
    bg, cg = b[...], c[...]
    inner = dot_nt(cg, bg)
    inner2 = jnp.concatenate([inner, inner], axis=1)
    row, col = iota((Q, 2 * Q), 0), iota((Q, 2 * Q), 1)
    causal = row >= lax.rem(col, Q)
    first = iota((Q, 2 * P_SIZE), 1) < P_SIZE
    m1 = first.astype(F32).astype(BF)
    m2 = 1 - m1
    total = jnp.zeros((Q, Q), F32)
    for j in range(PER_GROUP // 2):
        lanes = slice(j * 2 * P_SIZE, (j + 1) * 2 * P_SIZE)
        xp, dyp = x[:, lanes], dy[:, lanes]
        xbd = jnp.concatenate([xp * m1, xp * m2], axis=0)
        diff = jnp.concatenate(
            [
                run[0, :, 2 * j + i : 2 * j + i + 1] - runt[2 * j + i : 2 * j + i + 1, :]
                for i in range(2)
            ],
            axis=1,
        )
        dec = jnp.exp(jnp.where(causal, diff, -1e30))
        ad = dot_nt(dyp, xbd) * dec
        total = total + ad[:, :Q] + ad[:, Q:]
        mix = (dec * inner2).astype(BF)
        direct_o[:, lanes] = dot(mix, xbd)
        both = dot_tn(mix, dyp)
        gdirect_o[:, lanes] = jnp.where(first, both[:Q], both[Q:])
    grad_inner = total.astype(BF)
    gc_o[...] = dot(grad_inner, bg)
    gb_o[...] = dot_tn(grad_inner, cg)


def scan_kernel(msgs, out):
    count, _, width = msgs.shape

    def decay(k):
        tail = msgs[k, 2 * N :, :].astype(F32)
        return tail[0:1, :] + tail[8:9, :]

    carry = jnp.zeros((N, width), F32)
    for k in range(count):
        out[k, :N, :] = carry.astype(BF)
        if k < count - 1:
            carry = decay(k) * carry + msgs[k, :N, :].astype(F32)
    back = jnp.zeros((N, width), F32)
    for k in range(count - 1, -1, -1):
        out[k, N:, :] = back.astype(BF)
        if k > 0:
            back = decay(k) * back + msgs[k, N : 2 * N, :].astype(F32)


def finish_kernel(part, *refs):
    states, x, dy, b, c, run, skip, direct, gdirect, gc_i, gb_i = refs[:11]
    out_o, gx_o, gb_o, gc_o, gr_o = refs[-5:]
    e = expander()
    r = run[0]
    weight = expand(jnp.exp(r[Q - 1 :, :] - r), e)
    early = expand(jnp.exp(r), e)
    gain = expand(jnp.broadcast_to(skip[0], (8, PER_GROUP)), e)[0:1, :]
    carry = jnp.concatenate([states[k, :N, :] for k in range(states.shape[0])], axis=1)
    back = jnp.concatenate([states[k, N:, :] for k in range(states.shape[0])], axis=1)
    xg, dyg = x[...].astype(F32), dy[...].astype(F32)
    y = direct[...] + early * dot(c[...], carry)
    out_o[...] = (y + gain * xg).astype(BF)
    lateral = weight * dot(b[...], back)
    gx = gdirect[...] + lateral
    gx_o[...] = (gx + gain * dyg).astype(BF)
    gc_o[...] = (gc_i[...] + dot_nt((dyg * early).astype(BF), carry)).astype(BF)
    gb_o[...] = (gb_i[...] + dot_nt((xg * weight).astype(BF), back)).astype(BF)
    closing = jnp.sum(xg * lateral, axis=0, keepdims=True) + early[Q - 1 :, :] * jnp.sum(
        carry.astype(F32) * back.astype(F32), axis=0, keepdims=True
    )
    terms = dyg * y - xg * gx + jnp.where(iota((Q, GW), 0) == Q - 1, closing, 0.0)
    hi, lo = split2(terms)
    gr_o[0] = dot_nt(hi, e) + dot_nt(lo, e)


def raw_kernel(step, rate, *refs):
    raw_o, rawt_o = refs[-2:]
    grad_running = jnp.concatenate([gr[k] for gr in refs[:-2] for k in range(PG)], axis=1)
    gate = scan_dot(tri(False), grad_running)
    raw = gate * -rate[...] * jax.nn.sigmoid(step[...])
    raw_o[...] = raw.astype(BF)
    rawt = jnp.swapaxes(raw, 0, 1).astype(BF)
    for k in range(rawt_o.shape[0]):
        rawt_o[k] = rawt


def deal_kernel(idx, li_own, li_oth, *outs):
    count = len(outs)
    rows = outs[0].shape[1]
    per = count // 2
    for s, out in enumerate(outs):
        k = lax.rem(idx[1] + s, count)
        cols = pl.ds(pl.multiple_of(lax.rem(k, per) * rows, rows), rows)

        @pl.when(k // per == idx[0])
        def _():
            out[...] = li_own[:, cols]

        @pl.when(k // per != idx[0])
        def _():
            out[...] = li_oth[:, cols]


def rows_kernel(idx, rawt, *refs):
    out = refs[-1]
    count = len(refs) - 1
    total = jnp.zeros(out.shape, F32)
    for s in range(count):
        total = total + dot(rawt[lax.rem(idx[1] - s + count, count)], refs[s][...])
    out[...] = total.astype(out.dtype)


def add_kernel(*refs):
    a, b, c, d = (ref[...].astype(F32) for ref in refs[:-1])
    refs[-1][...] = ((a + c) + (b + d)).astype(refs[-1].dtype)


def input_kernel(idx, raw, raw_oth, w, w_oth, out):
    per, _, rows = w_oth.shape
    for k in range(per):
        out[:, k * rows : (k + 1) * rows] = (
            dot(raw[...], w[idx[0] * per + k]) + dot(raw_oth[...], w_oth[k])
        ).astype(BF)


SMEM_SPEC = pl.BlockSpec(memory_space=pltpu.SMEM)
VMEM_SPEC = pl.BlockSpec(memory_space=pltpu.VMEM)


def sds(shape, dtype):
    return jax.ShapeDtypeStruct(shape, dtype)


def call(kernel, name, outs, *args, scratch=(), scalars=0, vmem=SMALL):
    params = pltpu.CompilerParams(vmem_limit_bytes=vmem)
    return pl.pallas_call(
        kernel,
        out_shape=outs,
        in_specs=[SMEM_SPEC] * scalars + [VMEM_SPEC] * (len(args) - scalars),
        out_specs=jax.tree.map(lambda _: VMEM_SPEC, outs),
        scratch_shapes=list(scratch),
        compiler_params=params,
        name=name,
    )(*args)


def columns(width, first=0):
    return pl.BlockSpec((Q, width), lambda g: (0, g + first))


def heads_of(first=0):
    return pl.BlockSpec((1, Q, PER_GROUP), lambda g: (g + first, 0, 0))


def shards(
    layer_input, w_step, step_bias, decay_rate, ssm_input, b_input, c_input, skip_gain, grad_y
):
    dp, ctx = lax.axis_size("dp"), lax.axis_size("ctx")
    nz = GROUPS
    ny = ctx // nz
    me = lax.axis_index("head")
    idx = jnp.stack([me, lax.axis_index("dp")]).astype(jnp.int32)
    swap = [(0, 1), (1, 0)]
    params = pltpu.CompilerParams(vmem_limit_bytes=LARGE)

    def z_shift(v, s):
        pairs = [(y * nz + k, y * nz + (k + s) % nz) for y in range(ny) for k in range(nz)]
        return lax.ppermute(v, "ctx", pairs)

    def y_shift(v, s):
        pairs = [(y * nz + k, (y + s) % ny * nz + k) for y in range(ny) for k in range(nz)]
        return lax.ppermute(v, "ctx", pairs)

    li = layer_input[0]
    x, dy, b, c = ssm_input[0], grad_y[0], b_input[0], c_input[0]
    half = li.shape[1]
    rows = w_step.shape[0]
    per = half // rows
    bias, rate = step_bias.reshape(1, HEADS), decay_rate.reshape(1, HEADS)
    skip = skip_gain.reshape(GROUPS, 1, PER_GROUP)

    li_oth = lax.ppermute(li, "head", swap)
    w = lax.all_gather(w_step.T, "dp")
    step, run, runt = call(
        gates_kernel,
        "gates",
        [sds((Q, HEADS), F32), sds((GROUPS, Q, PER_GROUP), F32), sds((HEADS, Q), F32)],
        idx, li, li_oth, w, bias, rate,
        scalars=1,
    )

    width = PG * GW // ctx
    shares = GW // width
    sent = []
    for part in range(PARTS):
        at = part * PG
        sent.append(
            pl.pallas_call(
                pieces_kernel,
                grid=(PG,),
                out_shape=sds((ctx, ROWS, width), BF),
                in_specs=[columns(GW, at), columns(GW, at), columns(N, at), columns(N, at), heads_of(at)],
                out_specs=pl.BlockSpec((shares, ROWS, width), lambda g: (g, 0, 0)),
                compiler_params=pltpu.CompilerParams(vmem_limit_bytes=SMALL),
                name=f"pieces{part}",
            )(x, dy, b, c, run)
        )
    got = [lax.all_to_all(v, "ctx", 0, 0, tiled=True) for v in sent]

    w_oth = lax.ppermute(lax.dynamic_slice_in_dim(w, (1 - me) * per, per, 0), "head", swap)
    dealt = call(deal_kernel, "deal", [sds((Q, rows), BF)] * dp, idx, li, li_oth, scalars=1)
    li_rows = [dealt[0]] + [
        lax.ppermute(dealt[s], "dp", [(k, (k + s) % dp) for k in range(dp)]) for s in range(1, dp)
    ]

    direct, gdirect, gc, gb = pl.pallas_call(
        local_kernel,
        grid=(GROUPS,),
        out_shape=[
            sds((Q, GROUPS * GW), F32),
            sds((Q, GROUPS * GW), F32),
            sds((Q, GROUPS * N), F32),
            sds((Q, GROUPS * N), F32),
        ],
        in_specs=[
            columns(GW), columns(GW), columns(N), columns(N), heads_of(),
            pl.BlockSpec((PER_GROUP, Q), lambda g: (g, 0)),
        ],
        out_specs=[columns(GW), columns(GW), columns(N), columns(N)],
        compiler_params=params,
        cost_estimate=pl.CostEstimate(
            flops=4_000_000_000, bytes_accessed=12_000_000, transcendentals=1_100_000
        ),
        name="local",
    )(x, dy, b, c, run, runt)

    states = []
    for part in range(PARTS):
        back = call(scan_kernel, f"scan{part}", sds((ctx, 2 * N, width), BF), got[part])
        states.append(lax.all_to_all(back, "ctx", 0, 0, tiled=True))

    outs = []
    grads = []
    for part in range(PARTS):
        at = part * PG
        args = [states[part], x, dy, b, c, run, skip, direct, gdirect, gc, gb]
        *outs, gr = pl.pallas_call(
            functools.partial(finish_kernel, part),
            grid=(PG,),
            out_shape=[
                sds((Q, GROUPS * GW), BF),
                sds((Q, GROUPS * GW), BF),
                sds((Q, GROUPS * N), BF),
                sds((Q, GROUPS * N), BF),
                sds((PG, Q, PER_GROUP), F32),
            ],
            in_specs=[
                pl.BlockSpec((shares, 2 * N, width), lambda g: (g, 0, 0)),
                columns(GW, at), columns(GW, at), columns(N, at), columns(N, at), heads_of(at),
                pl.BlockSpec((1, 1, PER_GROUP), lambda g, at=at: (g + at, 0, 0)),
                columns(GW, at), columns(GW, at), columns(N, at), columns(N, at),
            ]
            + [pl.BlockSpec(memory_space=pl.ANY)] * len(outs),
            out_specs=[columns(GW, at), columns(GW, at), columns(N, at), columns(N, at), heads_of()],
            input_output_aliases={len(args) + k: k for k in range(len(outs))},
            compiler_params=params,
            cost_estimate=pl.CostEstimate(
                flops=1_000_000_000, bytes_accessed=6_000_000, transcendentals=100_000
            ),
            name=f"finish{part}",
        )(*args, *outs)
        grads.append(gr)
    output, grad_x, grad_b, grad_c = outs

    raw, rawt = call(
        raw_kernel, "raw", [sds((Q, HEADS), BF), sds((dp, HEADS, Q), BF)], step, rate, *grads
    )
    raw_oth = lax.ppermute(raw, "head", swap)
    rawt = lax.all_to_all(rawt, "dp", 0, 0, tiled=True)
    share = call(rows_kernel, "rows", sds((HEADS, rows), BF), idx, rawt, *li_rows, scalars=1, vmem=LARGE)
    share = call(
        add_kernel, "add_z", sds((HEADS, rows), BF),
        share, *[z_shift(share, s) for s in range(1, nz)],
    )
    grad_w = call(
        add_kernel, "add_y", sds((HEADS, rows), F32),
        share, *[y_shift(share, s) for s in range(1, ny)],
    )
    grad_input = call(
        input_kernel, "input", sds((Q, half), BF), idx, raw, raw_oth, w, w_oth, scalars=1
    )
    return output[None], grad_x[None], grad_b[None], grad_c[None], grad_input[None], grad_w.T


def solution(mesh):
    tokens = P("dp", "ctx", "head")
    in_specs = (
        tokens, P("dp", "head"), P("head"), P("head"), tokens, tokens, tokens, P("head"), tokens,
    )
    out_specs = (tokens, tokens, tokens, tokens, tokens, P("dp", "head"))
    return jax.shard_map(shards, mesh=mesh, in_specs=in_specs, out_specs=out_specs, check_vma=False)
```

```python
import jax
import jax.numpy as jnp
from jax import lax
from jax.experimental import pallas as pl
from jax.experimental.pallas import tpu as pltpu
from jax.sharding import PartitionSpec as P

BF = jnp.bfloat16
F32 = jnp.float32
P_SIZE = 64
N = 128
Q = 128
PER_GROUP = 16
GROUPS = 4
HEADS = GROUPS * PER_GROUP
GW = PER_GROUP * P_SIZE
TAIL = 16
LANES = 128
SMALL = 20 * 1024 * 1024
LARGE = 56 * 1024 * 1024


def dot(a, b):
    return jnp.dot(a, b, preferred_element_type=F32)


def dot_nt(a, b):
    return lax.dot_general(a, b, (((1,), (1,)), ((), ())), preferred_element_type=F32)


def dot_tn(a, b):
    return lax.dot_general(a, b, (((0,), (0,)), ((), ())), preferred_element_type=F32)


def split2(v):
    hi = v.astype(BF)
    return hi, (v - hi.astype(F32)).astype(BF)


def split3(v):
    hi = v.astype(BF)
    rest = v - hi.astype(F32)
    mid = rest.astype(BF)
    return hi, mid, (rest - mid.astype(F32)).astype(BF)


def iota(shape, dim):
    return lax.broadcasted_iota(jnp.int32, shape, dim)


def expander():
    return (iota((PER_GROUP, GW), 1) // P_SIZE == iota((PER_GROUP, GW), 0)).astype(F32).astype(BF)


def expand(v, e):
    return dot(jnp.concatenate(split2(v), axis=1), jnp.concatenate([e, e], axis=0))


def head_sums(v, e):
    hi, lo = split2(v)
    return dot_nt(hi, e) + dot_nt(lo, e)


def tri(lower):
    row, col = iota((Q, Q), 0), iota((Q, Q), 1)
    keep = row >= col if lower else row <= col
    return keep.astype(F32).astype(BF)


def scan_dot(t, v):
    a, b, c = split3(v)
    return dot(t, a) + dot(t, b) + dot(t, c)


def softplus(v):
    return jnp.maximum(v, 0.0) + jnp.log1p(jnp.exp(-jnp.abs(v)))


def front_kernel(
    idx, bias, rate, w_h, oth_h, li_h, x_h, dy_h, b_h, c_h, out, step_o, run_o, runt_o,
    w, li_oth, li_own, x, dy, b, c, sems,
):
    pairs = (
        (w_h, w), (oth_h, li_oth), (li_h, li_own), (b_h, b), (c_h, c), (x_h, x), (dy_h, dy)
    )
    loads = [pltpu.make_async_copy(*pair, sems.at[k]) for k, pair in enumerate(pairs)]
    for load in loads:
        load.start()
    loads[0].wait()
    loads[1].wait()
    count, _, rows = w.shape
    per = count // 2
    step = bias[...]
    for k in range(per):
        step = step + dot_nt(li_oth[:, k * rows : (k + 1) * rows], w[(1 - idx[0]) * per + k])
    loads[2].wait()
    for k in range(per):
        step = step + dot_nt(li_own[:, k * rows : (k + 1) * rows], w[idx[0] * per + k])
    step_o[...] = step
    running = scan_dot(tri(True), -rate[...] * softplus(step))
    runt_o[...] = jnp.swapaxes(running, 0, 1)
    e = expander()
    row = iota((TAIL, LANES), 0)
    _, total, _ = out.shape
    cuts = (total - TAIL) // (2 * N)
    shares = GW // (cuts * LANES)
    for load in loads[3:]:
        load.wait()
    for g in range(GROUPS):
        r = running[:, g * PER_GROUP : (g + 1) * PER_GROUP]
        run_o[g] = r
        weight = expand(jnp.exp(r[Q - 1 :, :] - r), e)
        early = expand(jnp.exp(r), e)
        wide, slim = slice(g * GW, (g + 1) * GW), slice(g * N, (g + 1) * N)
        scaled = (x[:, wide].astype(F32) * weight).astype(BF)
        scaled_dy = (dy[:, wide].astype(F32) * early).astype(BF)
        piece = dot_tn(b[:, slim], scaled).astype(BF)
        jump = dot_tn(c[:, slim], scaled_dy).astype(BF)
        last = early[Q - 1 :, :]
        rest = last - last.astype(BF).astype(F32)
        for k in range(shares):
            tail = jnp.zeros((TAIL, LANES), F32)
            to = g * shares + k
            for i in range(cuts):
                lanes = slice((k * cuts + i) * LANES, (k * cuts + i + 1) * LANES)
                at = i * 2 * N
                out[to, at : at + N, :] = piece[:, lanes]
                out[to, at + N : at + 2 * N, :] = jump[:, lanes]
                tail = jnp.where(row == 2 * i, last[:, lanes], tail)
                tail = jnp.where(row == 2 * i + 1, rest[:, lanes], tail)
            out[to, total - TAIL :, :] = tail.astype(BF)


def local_kernel(x, dy, b, c, run, runt, direct_o, gdirect_o, gc_o, gb_o, gr_o):
    bg, cg = b[...], c[...]
    inner = dot_nt(cg, bg)
    inner2 = jnp.concatenate([inner, inner], axis=1)
    row, col = iota((Q, 2 * Q), 0), iota((Q, 2 * Q), 1)
    causal = row >= lax.rem(col, Q)
    first = iota((Q, 2 * P_SIZE), 1) < P_SIZE
    m1 = first.astype(F32).astype(BF)
    m2 = 1 - m1
    total = jnp.zeros((Q, Q), F32)
    for j in range(PER_GROUP // 2):
        lanes = slice(j * 2 * P_SIZE, (j + 1) * 2 * P_SIZE)
        xp, dyp = x[:, lanes], dy[:, lanes]
        xbd = jnp.concatenate([xp * m1, xp * m2], axis=0)
        diff = jnp.concatenate(
            [
                run[0, :, 2 * j + i : 2 * j + i + 1] - runt[2 * j + i : 2 * j + i + 1, :]
                for i in range(2)
            ],
            axis=1,
        )
        dec = jnp.exp(jnp.where(causal, diff, -1e30))
        ad = dot_nt(dyp, xbd) * dec
        total = total + ad[:, :Q] + ad[:, Q:]
        mix = (dec * inner2).astype(BF)
        direct_o[:, lanes] = dot(mix, xbd)
        both = dot_tn(mix, dyp)
        gdirect_o[:, lanes] = jnp.where(first, both[:Q], both[Q:])
    grad_inner = total.astype(BF)
    gc_o[...] = dot(grad_inner, bg)
    gb_o[...] = dot_tn(grad_inner, cg)
    gr_o[0] = head_sums(
        dy[...].astype(F32) * direct_o[...] - x[...].astype(F32) * gdirect_o[...], expander()
    )


def scan_kernel(msgs, out):
    count, total, _ = msgs.shape
    for i in range((total - TAIL) // (2 * N)):
        at = i * 2 * N

        def decay(k):
            tail = msgs[k, total - TAIL :, :].astype(F32)
            return tail[2 * i : 2 * i + 1, :] + tail[2 * i + 1 : 2 * i + 2, :]

        carry = jnp.zeros((N, LANES), F32)
        for k in range(count):
            out[k, at : at + N, :] = carry.astype(BF)
            if k < count - 1:
                carry = decay(k) * carry + msgs[k, at : at + N, :].astype(F32)
        back = jnp.zeros((N, LANES), F32)
        for k in range(count - 1, -1, -1):
            out[k, at + N : at + 2 * N, :] = back.astype(BF)
            if k > 0:
                back = decay(k) * back + msgs[k, at + N : at + 2 * N, :].astype(F32)


def states_of(states):
    shares, total, _ = states.shape
    starts = [(k, at) for k in range(shares) for at in range(0, total, 2 * N)]
    carry = jnp.concatenate([states[k, at : at + N, :] for k, at in starts], axis=1)
    back = jnp.concatenate([states[k, at + N : at + 2 * N, :] for k, at in starts], axis=1)
    return carry, back


def raw_kernel(states, x, dy, b, c, run, gr_i, step, rate, raw_o, rawt_o, gr):
    g = pl.program_id(0)
    e = expander()
    r = run[0]
    closing = r[Q - 1 :, :]
    carry, back = states_of(states)
    fore = head_sums(dy[...].astype(F32) * dot(c[...], carry), e)
    aft = jnp.exp(closing - r) * head_sums(x[...].astype(F32) * dot(b[...], back), e)
    both = jnp.sum(carry.astype(F32) * back.astype(F32), axis=0, keepdims=True)
    both = head_sums(jnp.broadcast_to(both, (8, GW)), e)[0:1, :]
    end = jnp.sum(aft, axis=0, keepdims=True) + jnp.exp(closing) * both
    gr[g] = (
        gr_i[0] + jnp.exp(r) * fore - aft + jnp.where(iota((Q, PER_GROUP), 0) == Q - 1, end, 0.0)
    )

    @pl.when(g == GROUPS - 1)
    def _():
        grad_running = jnp.concatenate([gr[k] for k in range(GROUPS)], axis=1)
        gate = scan_dot(tri(False), grad_running)
        raw = gate * -rate[...] * jax.nn.sigmoid(step[...])
        raw_o[...] = raw.astype(BF)
        rawt = jnp.swapaxes(raw, 0, 1).astype(BF)
        for k in range(rawt_o.shape[0]):
            rawt_o[k] = rawt


def finish_kernel(
    states, x, dy, b, c, run, skip, direct, gdirect, gc_i, gb_i, out_o, gx_o, gb_o, gc_o
):
    e = expander()
    r = run[0]
    weight = expand(jnp.exp(r[Q - 1 :, :] - r), e)
    early = expand(jnp.exp(r), e)
    gain = expand(jnp.broadcast_to(skip[0], (8, PER_GROUP)), e)[0:1, :]
    carry, back = states_of(states)
    xg, dyg = x[...].astype(F32), dy[...].astype(F32)
    out_o[...] = (direct[...] + early * dot(c[...], carry) + gain * xg).astype(BF)
    gx_o[...] = (gdirect[...] + weight * dot(b[...], back) + gain * dyg).astype(BF)
    gc_o[...] = (gc_i[...] + dot_nt((dyg * early).astype(BF), carry)).astype(BF)
    gb_o[...] = (gb_i[...] + dot_nt((xg * weight).astype(BF), back)).astype(BF)


def deal_kernel(idx, li_own, li_oth, *outs):
    count = len(outs)
    rows = outs[0].shape[1]
    per = count // 2
    for s, out in enumerate(outs):
        k = lax.rem(idx[1] + s, count)
        cols = pl.ds(pl.multiple_of(lax.rem(k, per) * rows, rows), rows)

        @pl.when(k // per == idx[0])
        def _():
            out[...] = li_own[:, cols]

        @pl.when(k // per != idx[0])
        def _():
            out[...] = li_oth[:, cols]


def rows_kernel(idx, rawt, *refs):
    out = refs[-1]
    count = len(refs) - 1
    total = jnp.zeros(out.shape, F32)
    for s in range(count):
        total = total + dot(rawt[lax.rem(idx[1] - s + count, count)], refs[s][...])
    out[...] = total.astype(out.dtype)


def add_kernel(*refs):
    a, b, c, d = (ref[...].astype(F32) for ref in refs[:-1])
    refs[-1][...] = ((a + c) + (b + d)).astype(refs[-1].dtype)


def input_kernel(idx, raw, raw_oth, w, w_oth, out):
    per, _, rows = w_oth.shape
    for k in range(per):
        out[:, k * rows : (k + 1) * rows] = (
            dot(raw[...], w[idx[0] * per + k]) + dot(raw_oth[...], w_oth[k])
        ).astype(BF)


SMEM_SPEC = pl.BlockSpec(memory_space=pltpu.SMEM)
VMEM_SPEC = pl.BlockSpec(memory_space=pltpu.VMEM)


def sds(shape, dtype):
    return jax.ShapeDtypeStruct(shape, dtype)


def call(kernel, name, outs, *args, scratch=(), scalars=0, vmem=SMALL):
    params = pltpu.CompilerParams(vmem_limit_bytes=vmem)
    return pl.pallas_call(
        kernel,
        out_shape=outs,
        in_specs=[SMEM_SPEC] * scalars + [VMEM_SPEC] * (len(args) - scalars),
        out_specs=jax.tree.map(lambda _: VMEM_SPEC, outs),
        scratch_shapes=list(scratch),
        compiler_params=params,
        name=name,
    )(*args)


def columns(width, first=0):
    return pl.BlockSpec((Q, width), lambda g: (0, g + first))


def heads_of(first=0):
    return pl.BlockSpec((1, Q, PER_GROUP), lambda g: (g + first, 0, 0))


def shards(
    layer_input, w_step, step_bias, decay_rate, ssm_input, b_input, c_input, skip_gain, grad_y
):
    dp, ctx = lax.axis_size("dp"), lax.axis_size("ctx")
    nz = GROUPS
    ny = ctx // nz
    me = lax.axis_index("head")
    idx = jnp.stack([me, lax.axis_index("dp")]).astype(jnp.int32)
    swap = [(0, 1), (1, 0)]
    params = pltpu.CompilerParams(vmem_limit_bytes=LARGE)

    def z_shift(v, s):
        pairs = [(y * nz + k, y * nz + (k + s) % nz) for y in range(ny) for k in range(nz)]
        return lax.ppermute(v, "ctx", pairs)

    def y_shift(v, s):
        pairs = [(y * nz + k, (y + s) % ny * nz + k) for y in range(ny) for k in range(nz)]
        return lax.ppermute(v, "ctx", pairs)

    li = layer_input[0]
    x, dy, b, c = ssm_input[0], grad_y[0], b_input[0], c_input[0]
    half = li.shape[1]
    rows = w_step.shape[0]
    per = half // rows
    bias, rate = step_bias.reshape(1, HEADS), decay_rate.reshape(1, HEADS)
    skip = skip_gain.reshape(GROUPS, 1, PER_GROUP)

    li_oth = lax.ppermute(li, "head", swap)
    w = lax.all_gather(w_step.T, "dp")
    cuts = GROUPS * GW // (ctx * LANES)
    shares = GW // (cuts * LANES)
    total = cuts * 2 * N
    sent, step, run, runt = pl.pallas_call(
        front_kernel,
        out_shape=[
            sds((ctx, total + TAIL, LANES), BF),
            sds((Q, HEADS), F32),
            sds((GROUPS, Q, PER_GROUP), F32),
            sds((HEADS, Q), F32),
        ],
        in_specs=[SMEM_SPEC] + [VMEM_SPEC] * 2 + [pl.BlockSpec(memory_space=pl.ANY)] * 7,
        out_specs=[VMEM_SPEC] * 4,
        scratch_shapes=[
            pltpu.VMEM((dp, HEADS, rows), BF),
            pltpu.VMEM((Q, half), BF),
            pltpu.VMEM((Q, half), BF),
            pltpu.VMEM((Q, GROUPS * GW), BF),
            pltpu.VMEM((Q, GROUPS * GW), BF),
            pltpu.VMEM((Q, GROUPS * N), BF),
            pltpu.VMEM((Q, GROUPS * N), BF),
            pltpu.SemaphoreType.DMA((7,)),
        ],
        compiler_params=params,
        name="front",
    )(idx, bias, rate, w, li_oth, li, x, dy, b, c)
    got = lax.all_to_all(sent, "ctx", 0, 0, tiled=True)

    w_oth = lax.ppermute(lax.dynamic_slice_in_dim(w, (1 - me) * per, per, 0), "head", swap)
    dealt = call(deal_kernel, "deal", [sds((Q, rows), BF)] * dp, idx, li, li_oth, scalars=1)
    li_rows = [dealt[0]] + [
        lax.ppermute(dealt[s], "dp", [(k, (k + s) % dp) for k in range(dp)]) for s in range(1, dp)
    ]

    direct, gdirect, gc, gb, gr = pl.pallas_call(
        local_kernel,
        grid=(GROUPS,),
        out_shape=[
            sds((Q, GROUPS * GW), F32),
            sds((Q, GROUPS * GW), F32),
            sds((Q, GROUPS * N), F32),
            sds((Q, GROUPS * N), F32),
            sds((GROUPS, Q, PER_GROUP), F32),
        ],
        in_specs=[
            columns(GW), columns(GW), columns(N), columns(N), heads_of(),
            pl.BlockSpec((PER_GROUP, Q), lambda g: (g, 0)),
        ],
        out_specs=[columns(GW), columns(GW), columns(N), columns(N), heads_of()],
        compiler_params=params,
        cost_estimate=pl.CostEstimate(
            flops=4_000_000_000, bytes_accessed=12_000_000, transcendentals=1_100_000
        ),
        name="local",
    )(x, dy, b, c, run, runt)

    back = call(scan_kernel, "scan", sds((ctx, total, LANES), BF), got)
    states = lax.all_to_all(back, "ctx", 0, 0, tiled=True)
    states, li_rows = lax.optimization_barrier((states, li_rows))
    state_spec = pl.BlockSpec((shares, total, LANES), lambda g: (g, 0, 0))
    whole = lambda *shape: pl.BlockSpec(shape, lambda g: (0,) * len(shape))

    raw, rawt = pl.pallas_call(
        raw_kernel,
        grid=(GROUPS,),
        out_shape=[sds((Q, HEADS), BF), sds((dp, HEADS, Q), BF)],
        in_specs=[
            state_spec, columns(GW), columns(GW), columns(N), columns(N), heads_of(), heads_of(),
            whole(Q, HEADS), whole(1, HEADS),
        ],
        out_specs=[whole(Q, HEADS), whole(dp, HEADS, Q)],
        scratch_shapes=[pltpu.VMEM((GROUPS, Q, PER_GROUP), F32)],
        compiler_params=params,
        name="raw",
    )(states, x, dy, b, c, run, gr, step, rate)

    outs = pl.pallas_call(
        finish_kernel,
        grid=(GROUPS,),
        out_shape=[
            sds((Q, GROUPS * GW), BF),
            sds((Q, GROUPS * GW), BF),
            sds((Q, GROUPS * N), BF),
            sds((Q, GROUPS * N), BF),
        ],
        in_specs=[
            state_spec, columns(GW), columns(GW), columns(N), columns(N), heads_of(),
            pl.BlockSpec((1, 1, PER_GROUP), lambda g: (g, 0, 0)),
            columns(GW), columns(GW), columns(N), columns(N),
        ],
        out_specs=[columns(GW), columns(GW), columns(N), columns(N)],
        compiler_params=params,
        cost_estimate=pl.CostEstimate(
            flops=4_000_000_000, bytes_accessed=12_000_000, transcendentals=200_000
        ),
        name="finish",
    )(states, x, dy, b, c, run, skip, direct, gdirect, gc, gb)

    raw_oth = lax.ppermute(raw, "head", swap)
    grad_input = call(
        input_kernel, "input", sds((Q, half), BF), idx, raw, raw_oth, w, w_oth, scalars=1
    )
    rawt = lax.all_to_all(rawt, "dp", 0, 0, tiled=True)
    rawt, grad_input = lax.optimization_barrier((rawt, grad_input))
    share = call(rows_kernel, "rows", sds((HEADS, rows), BF), idx, rawt, *li_rows, scalars=1, vmem=LARGE)
    near = [z_shift(share, s) for s in range(1, nz)]
    near, outs = lax.optimization_barrier((near, outs))
    output, grad_x, grad_b, grad_c = outs
    share = call(add_kernel, "add_z", sds((HEADS, rows), BF), share, *near)
    grad_w = call(
        add_kernel, "add_y", sds((HEADS, rows), F32),
        share, *[y_shift(share, s) for s in range(1, ny)],
    )
    return output[None], grad_x[None], grad_b[None], grad_c[None], grad_input[None], grad_w.T


def solution(mesh):
    tokens = P("dp", "ctx", "head")
    in_specs = (
        tokens, P("dp", "head"), P("head"), P("head"), tokens, tokens, tokens, P("head"), tokens,
    )
    out_specs = (tokens, tokens, tokens, tokens, tokens, P("dp", "head"))
    return jax.shard_map(shards, mesh=mesh, in_specs=in_specs, out_specs=out_specs, check_vma=False)
```

```python
import jax
import jax.numpy as jnp
from jax import lax
from jax.experimental import pallas as pl
from jax.experimental.pallas import tpu as pltpu
from jax.sharding import PartitionSpec as P

BF = jnp.bfloat16
F32 = jnp.float32
P_SIZE = 64
N = 128
Q = 128
PER_GROUP = 16
GROUPS = 4
HEADS = GROUPS * PER_GROUP
GW = PER_GROUP * P_SIZE
TAIL = 16
LANES = 128
SMALL = 20 * 1024 * 1024
LARGE = 56 * 1024 * 1024


def dot(a, b):
    return jnp.dot(a, b, preferred_element_type=F32)


def dot_nt(a, b):
    return lax.dot_general(a, b, (((1,), (1,)), ((), ())), preferred_element_type=F32)


def dot_tn(a, b):
    return lax.dot_general(a, b, (((0,), (0,)), ((), ())), preferred_element_type=F32)


def split2(v):
    hi = v.astype(BF)
    return hi, (v - hi.astype(F32)).astype(BF)


def split3(v):
    hi = v.astype(BF)
    rest = v - hi.astype(F32)
    mid = rest.astype(BF)
    return hi, mid, (rest - mid.astype(F32)).astype(BF)


def iota(shape, dim):
    return lax.broadcasted_iota(jnp.int32, shape, dim)


def expander():
    return (iota((PER_GROUP, GW), 1) // P_SIZE == iota((PER_GROUP, GW), 0)).astype(F32).astype(BF)


def expand(v, e):
    return dot(jnp.concatenate(split2(v), axis=1), jnp.concatenate([e, e], axis=0))


def head_sums(v, e):
    hi, lo = split2(v)
    return dot_nt(hi, e) + dot_nt(lo, e)


def tri(lower):
    row, col = iota((Q, Q), 0), iota((Q, Q), 1)
    keep = row >= col if lower else row <= col
    return keep.astype(F32).astype(BF)


def scan_dot(t, v):
    a, b, c = split3(v)
    return dot(t, a) + dot(t, b) + dot(t, c)


def softplus(v):
    return jnp.maximum(v, 0.0) + jnp.log1p(jnp.exp(-jnp.abs(v)))


def front_kernel(
    idx, bias, rate, oth_h, li_h, x_h, dy_h, b_h, c_h, *refs
):
    blocks, (out, step_o, run_o, runt_o, w, li_oth, li_own, x, dy, b, c, sems) = refs[:-12], refs[-12:]
    chips = len(blocks) // 2
    pairs = [(oth_h, li_oth), (li_h, li_own), (b_h, b), (c_h, c), (x_h, x), (dy_h, dy)]
    for s, block in enumerate(blocks):
        chip = lax.rem(idx[1] // 2 - s % chips + chips, chips)
        core = lax.rem(idx[1] + s // chips, 2)
        pairs.insert(s, (block, w.at[2 * chip + core]))
    loads = [pltpu.make_async_copy(*pair, sems.at[k]) for k, pair in enumerate(pairs)]
    for load in loads:
        load.start()
    for load in loads[:-5]:
        load.wait()
    count, _, rows = w.shape
    per = count // 2
    step = bias[...]
    for k in range(per):
        step = step + dot_nt(li_oth[:, k * rows : (k + 1) * rows], w[(1 - idx[0]) * per + k])
    loads[-5].wait()
    for k in range(per):
        step = step + dot_nt(li_own[:, k * rows : (k + 1) * rows], w[idx[0] * per + k])
    step_o[...] = step
    running = scan_dot(tri(True), -rate[...] * softplus(step))
    runt_o[...] = jnp.swapaxes(running, 0, 1)
    e = expander()
    row = iota((TAIL, LANES), 0)
    _, total, _ = out.shape
    cuts = (total - TAIL) // (2 * N)
    shares = GW // (cuts * LANES)
    for load in loads[-4:]:
        load.wait()
    for g in range(GROUPS):
        r = running[:, g * PER_GROUP : (g + 1) * PER_GROUP]
        run_o[g] = r
        weight = expand(jnp.exp(r[Q - 1 :, :] - r), e)
        early = expand(jnp.exp(r), e)
        wide, slim = slice(g * GW, (g + 1) * GW), slice(g * N, (g + 1) * N)
        scaled = (x[:, wide].astype(F32) * weight).astype(BF)
        scaled_dy = (dy[:, wide].astype(F32) * early).astype(BF)
        piece = dot_tn(b[:, slim], scaled).astype(BF)
        jump = dot_tn(c[:, slim], scaled_dy).astype(BF)
        last = early[Q - 1 :, :]
        rest = last - last.astype(BF).astype(F32)
        for k in range(shares):
            tail = jnp.zeros((TAIL, LANES), F32)
            to = g * shares + k
            for i in range(cuts):
                lanes = slice((k * cuts + i) * LANES, (k * cuts + i + 1) * LANES)
                at = i * 2 * N
                out[to, at : at + N, :] = piece[:, lanes]
                out[to, at + N : at + 2 * N, :] = jump[:, lanes]
                tail = jnp.where(row == 2 * i, last[:, lanes], tail)
                tail = jnp.where(row == 2 * i + 1, rest[:, lanes], tail)
            out[to, total - TAIL :, :] = tail.astype(BF)


def local_kernel(x, dy, b, c, run, runt, direct_o, gdirect_o, gc_o, gb_o, gr_o):
    bg, cg = b[...], c[...]
    inner = dot_nt(cg, bg)
    inner2 = jnp.concatenate([inner, inner], axis=1)
    row, col = iota((Q, 2 * Q), 0), iota((Q, 2 * Q), 1)
    causal = row >= lax.rem(col, Q)
    first = iota((Q, 2 * P_SIZE), 1) < P_SIZE
    m1 = first.astype(F32).astype(BF)
    m2 = 1 - m1
    total = jnp.zeros((Q, Q), F32)
    for j in range(PER_GROUP // 2):
        lanes = slice(j * 2 * P_SIZE, (j + 1) * 2 * P_SIZE)
        xp, dyp = x[:, lanes], dy[:, lanes]
        xbd = jnp.concatenate([xp * m1, xp * m2], axis=0)
        diff = jnp.concatenate(
            [
                run[0, :, 2 * j + i : 2 * j + i + 1] - runt[2 * j + i : 2 * j + i + 1, :]
                for i in range(2)
            ],
            axis=1,
        )
        dec = jnp.exp(jnp.where(causal, diff, -1e30))
        ad = dot_nt(dyp, xbd) * dec
        total = total + ad[:, :Q] + ad[:, Q:]
        mix = (dec * inner2).astype(BF)
        direct_o[:, lanes] = dot(mix, xbd)
        both = dot_tn(mix, dyp)
        gdirect_o[:, lanes] = jnp.where(first, both[:Q], both[Q:])
    grad_inner = total.astype(BF)
    gc_o[...] = dot(grad_inner, bg)
    gb_o[...] = dot_tn(grad_inner, cg)
    gr_o[0] = head_sums(
        dy[...].astype(F32) * direct_o[...] - x[...].astype(F32) * gdirect_o[...], expander()
    )


def scan_kernel(msgs, out):
    count, total, _ = msgs.shape
    for i in range((total - TAIL) // (2 * N)):
        at = i * 2 * N

        def decay(k):
            tail = msgs[k, total - TAIL :, :].astype(F32)
            return tail[2 * i : 2 * i + 1, :] + tail[2 * i + 1 : 2 * i + 2, :]

        carry = jnp.zeros((N, LANES), F32)
        for k in range(count):
            out[k, at : at + N, :] = carry.astype(BF)
            if k < count - 1:
                carry = decay(k) * carry + msgs[k, at : at + N, :].astype(F32)
        back = jnp.zeros((N, LANES), F32)
        for k in range(count - 1, -1, -1):
            out[k, at + N : at + 2 * N, :] = back.astype(BF)
            if k > 0:
                back = decay(k) * back + msgs[k, at + N : at + 2 * N, :].astype(F32)


def states_of(states):
    shares, total, _ = states.shape
    starts = [(k, at) for k in range(shares) for at in range(0, total, 2 * N)]
    carry = jnp.concatenate([states[k, at : at + N, :] for k, at in starts], axis=1)
    back = jnp.concatenate([states[k, at + N : at + 2 * N, :] for k, at in starts], axis=1)
    return carry, back


def raw_kernel(states, x, dy, b, c, run, gr_i, step, rate, raw_o, rawt_o, gr):
    g = pl.program_id(0)
    e = expander()
    r = run[0]
    closing = r[Q - 1 :, :]
    carry, back = states_of(states)
    fore = head_sums(dy[...].astype(F32) * dot(c[...], carry), e)
    aft = jnp.exp(closing - r) * head_sums(x[...].astype(F32) * dot(b[...], back), e)
    both = jnp.sum(carry.astype(F32) * back.astype(F32), axis=0, keepdims=True)
    both = head_sums(jnp.broadcast_to(both, (8, GW)), e)[0:1, :]
    end = jnp.sum(aft, axis=0, keepdims=True) + jnp.exp(closing) * both
    gr[g] = (
        gr_i[0] + jnp.exp(r) * fore - aft + jnp.where(iota((Q, PER_GROUP), 0) == Q - 1, end, 0.0)
    )

    @pl.when(g == GROUPS - 1)
    def _():
        grad_running = jnp.concatenate([gr[k] for k in range(GROUPS)], axis=1)
        gate = scan_dot(tri(False), grad_running)
        raw = gate * -rate[...] * jax.nn.sigmoid(step[...])
        raw_o[...] = raw.astype(BF)
        rawt = jnp.swapaxes(raw, 0, 1).astype(BF)
        for k in range(rawt_o.shape[0]):
            rawt_o[k] = rawt


def finish_kernel(
    states, x, dy, b, c, run, skip, direct, gdirect, gc_i, gb_i, out_o, gx_o, gb_o, gc_o
):
    e = expander()
    r = run[0]
    weight = expand(jnp.exp(r[Q - 1 :, :] - r), e)
    early = expand(jnp.exp(r), e)
    gain = expand(jnp.broadcast_to(skip[0], (8, PER_GROUP)), e)[0:1, :]
    carry, back = states_of(states)
    xg, dyg = x[...].astype(F32), dy[...].astype(F32)
    out_o[...] = (direct[...] + early * dot(c[...], carry) + gain * xg).astype(BF)
    gx_o[...] = (gdirect[...] + weight * dot(b[...], back) + gain * dyg).astype(BF)
    gc_o[...] = (gc_i[...] + dot_nt((dyg * early).astype(BF), carry)).astype(BF)
    gb_o[...] = (gb_i[...] + dot_nt((xg * weight).astype(BF), back)).astype(BF)


def deal_kernel(idx, li_own, li_oth, *outs):
    count = len(outs)
    rows = outs[0].shape[1]
    per = count // 2
    for s, out in enumerate(outs):
        k = lax.rem(idx[1] + s, count)
        cols = pl.ds(pl.multiple_of(lax.rem(k, per) * rows, rows), rows)

        @pl.when(k // per == idx[0])
        def _():
            out[...] = li_own[:, cols]

        @pl.when(k // per != idx[0])
        def _():
            out[...] = li_oth[:, cols]


def rows_kernel(idx, rawt, *refs):
    out = refs[-1]
    count = len(refs) - 1
    total = jnp.zeros(out.shape, F32)
    for s in range(count):
        total = total + dot(rawt[lax.rem(idx[1] - s + count, count)], refs[s][...])
    out[...] = total.astype(out.dtype)


def add_kernel(*refs):
    a, b, c, d = (ref[...].astype(F32) for ref in refs[:-1])
    refs[-1][...] = ((a + c) + (b + d)).astype(refs[-1].dtype)


def input_kernel(idx, raw, raw_oth, w, w_oth, out):
    per, _, rows = w_oth.shape
    for k in range(per):
        out[:, k * rows : (k + 1) * rows] = (
            dot(raw[...], w[idx[0] * per + k]) + dot(raw_oth[...], w_oth[k])
        ).astype(BF)


SMEM_SPEC = pl.BlockSpec(memory_space=pltpu.SMEM)
VMEM_SPEC = pl.BlockSpec(memory_space=pltpu.VMEM)


def sds(shape, dtype):
    return jax.ShapeDtypeStruct(shape, dtype)


def call(kernel, name, outs, *args, scratch=(), scalars=0, vmem=SMALL):
    params = pltpu.CompilerParams(vmem_limit_bytes=vmem)
    return pl.pallas_call(
        kernel,
        out_shape=outs,
        in_specs=[SMEM_SPEC] * scalars + [VMEM_SPEC] * (len(args) - scalars),
        out_specs=jax.tree.map(lambda _: VMEM_SPEC, outs),
        scratch_shapes=list(scratch),
        compiler_params=params,
        name=name,
    )(*args)


def columns(width, first=0):
    return pl.BlockSpec((Q, width), lambda g: (0, g + first))


def heads_of(first=0):
    return pl.BlockSpec((1, Q, PER_GROUP), lambda g: (g + first, 0, 0))


def shards(
    layer_input, w_step, step_bias, decay_rate, ssm_input, b_input, c_input, skip_gain, grad_y
):
    dp, ctx = lax.axis_size("dp"), lax.axis_size("ctx")
    nz = GROUPS
    ny = ctx // nz
    me = lax.axis_index("head")
    idx = jnp.stack([me, lax.axis_index("dp")]).astype(jnp.int32)
    swap = [(0, 1), (1, 0)]
    params = pltpu.CompilerParams(vmem_limit_bytes=LARGE)

    def z_shift(v, s):
        pairs = [(y * nz + k, y * nz + (k + s) % nz) for y in range(ny) for k in range(nz)]
        return lax.ppermute(v, "ctx", pairs)

    def y_shift(v, s):
        pairs = [(y * nz + k, (y + s) % ny * nz + k) for y in range(ny) for k in range(nz)]
        return lax.ppermute(v, "ctx", pairs)

    li = layer_input[0]
    x, dy, b, c = ssm_input[0], grad_y[0], b_input[0], c_input[0]
    half = li.shape[1]
    rows = w_step.shape[0]
    per = half // rows
    bias, rate = step_bias.reshape(1, HEADS), decay_rate.reshape(1, HEADS)
    skip = skip_gain.reshape(GROUPS, 1, PER_GROUP)

    li_oth = lax.ppermute(li, "head", swap)
    chips = dp // 2
    mine = [w_step.T]
    mine += [
        lax.ppermute(mine[0], "dp", [(k, (k + 2 * s) % dp) for k in range(dp)])
        for s in range(1, chips)
    ]
    w_blocks = mine + [lax.ppermute(v, "dp", [(k, k ^ 1) for k in range(dp)]) for v in mine]
    cuts = GROUPS * GW // (ctx * LANES)
    shares = GW // (cuts * LANES)
    total = cuts * 2 * N
    sent, step, run, runt, w = pl.pallas_call(
        front_kernel,
        out_shape=[
            sds((ctx, total + TAIL, LANES), BF),
            sds((Q, HEADS), F32),
            sds((GROUPS, Q, PER_GROUP), F32),
            sds((HEADS, Q), F32),
            sds((dp, HEADS, rows), BF),
        ],
        in_specs=[SMEM_SPEC] + [VMEM_SPEC] * 2 + [pl.BlockSpec(memory_space=pl.ANY)] * (6 + dp),
        out_specs=[VMEM_SPEC] * 5,
        scratch_shapes=[
            pltpu.VMEM((Q, half), BF),
            pltpu.VMEM((Q, half), BF),
            pltpu.VMEM((Q, GROUPS * GW), BF),
            pltpu.VMEM((Q, GROUPS * GW), BF),
            pltpu.VMEM((Q, GROUPS * N), BF),
            pltpu.VMEM((Q, GROUPS * N), BF),
            pltpu.SemaphoreType.DMA((6 + dp,)),
        ],
        compiler_params=params,
        name="front",
    )(idx, bias, rate, li_oth, li, x, dy, b, c, *w_blocks)
    got = lax.all_to_all(sent, "ctx", 0, 0, tiled=True)

    w_oth = lax.ppermute(lax.dynamic_slice_in_dim(w, (1 - me) * per, per, 0), "head", swap)
    dealt = call(deal_kernel, "deal", [sds((Q, rows), BF)] * dp, idx, li, li_oth, scalars=1)
    li_rows = [dealt[0]] + [
        lax.ppermute(dealt[s], "dp", [(k, (k + s) % dp) for k in range(dp)]) for s in range(1, dp)
    ]

    direct, gdirect, gc, gb, gr = pl.pallas_call(
        local_kernel,
        grid=(GROUPS,),
        out_shape=[
            sds((Q, GROUPS * GW), F32),
            sds((Q, GROUPS * GW), F32),
            sds((Q, GROUPS * N), F32),
            sds((Q, GROUPS * N), F32),
            sds((GROUPS, Q, PER_GROUP), F32),
        ],
        in_specs=[
            columns(GW), columns(GW), columns(N), columns(N), heads_of(),
            pl.BlockSpec((PER_GROUP, Q), lambda g: (g, 0)),
        ],
        out_specs=[columns(GW), columns(GW), columns(N), columns(N), heads_of()],
        compiler_params=params,
        cost_estimate=pl.CostEstimate(
            flops=4_000_000_000, bytes_accessed=12_000_000, transcendentals=1_100_000
        ),
        name="local",
    )(x, dy, b, c, run, runt)

    back = call(scan_kernel, "scan", sds((ctx, total, LANES), BF), got)
    states = lax.all_to_all(back, "ctx", 0, 0, tiled=True)
    states, li_rows, skip, w_oth = lax.optimization_barrier((states, li_rows, skip, w_oth))
    state_spec = pl.BlockSpec((shares, total, LANES), lambda g: (g, 0, 0))
    whole = lambda *shape: pl.BlockSpec(shape, lambda g: (0,) * len(shape))

    raw, rawt = pl.pallas_call(
        raw_kernel,
        grid=(GROUPS,),
        out_shape=[sds((Q, HEADS), BF), sds((dp, HEADS, Q), BF)],
        in_specs=[
            state_spec, columns(GW), columns(GW), columns(N), columns(N), heads_of(), heads_of(),
            whole(Q, HEADS), whole(1, HEADS),
        ],
        out_specs=[whole(Q, HEADS), whole(dp, HEADS, Q)],
        scratch_shapes=[pltpu.VMEM((GROUPS, Q, PER_GROUP), F32)],
        compiler_params=params,
        name="raw",
    )(states, x, dy, b, c, run, gr, step, rate)

    outs = pl.pallas_call(
        finish_kernel,
        grid=(GROUPS,),
        out_shape=[
            sds((Q, GROUPS * GW), BF),
            sds((Q, GROUPS * GW), BF),
            sds((Q, GROUPS * N), BF),
            sds((Q, GROUPS * N), BF),
        ],
        in_specs=[
            state_spec, columns(GW), columns(GW), columns(N), columns(N), heads_of(),
            pl.BlockSpec((1, 1, PER_GROUP), lambda g: (g, 0, 0)),
            columns(GW), columns(GW), columns(N), columns(N),
        ],
        out_specs=[columns(GW), columns(GW), columns(N), columns(N)],
        compiler_params=params,
        cost_estimate=pl.CostEstimate(
            flops=4_000_000_000, bytes_accessed=12_000_000, transcendentals=200_000
        ),
        name="finish",
    )(states, x, dy, b, c, run, skip, direct, gdirect, gc, gb)

    raw_oth = lax.ppermute(raw, "head", swap)
    rawt = lax.all_to_all(rawt, "dp", 0, 0, tiled=True)
    rawt, raw_oth = lax.optimization_barrier((rawt, raw_oth))
    share = call(rows_kernel, "rows", sds((HEADS, rows), BF), idx, rawt, *li_rows, scalars=1, vmem=LARGE)
    near = [z_shift(share, s) for s in range(1, nz)]
    near, outs = lax.optimization_barrier((near, outs))
    output, grad_x, grad_b, grad_c = outs
    share = call(add_kernel, "add_z", sds((HEADS, rows), BF), share, *near)
    grad_input = call(
        input_kernel, "input", sds((Q, half), BF), idx, raw, raw_oth, w, w_oth, scalars=1
    )
    near = [y_shift(share, s) for s in range(1, ny)]
    near, grad_input = lax.optimization_barrier((near, grad_input))
    grad_w = call(add_kernel, "add_y", sds((HEADS, rows), F32), share, *near)
    return output[None], grad_x[None], grad_b[None], grad_c[None], grad_input[None], grad_w.T


def solution(mesh):
    tokens = P("dp", "ctx", "head")
    in_specs = (
        tokens, P("dp", "head"), P("head"), P("head"), tokens, tokens, tokens, P("head"), tokens,
    )
    out_specs = (tokens, tokens, tokens, tokens, tokens, P("dp", "head"))
    return jax.shard_map(shards, mesh=mesh, in_specs=in_specs, out_specs=out_specs, check_vma=False)
```

```python
import jax
import jax.numpy as jnp
from jax import lax
from jax.experimental import pallas as pl
from jax.experimental.pallas import tpu as pltpu
from jax.sharding import PartitionSpec as P

BF = jnp.bfloat16
F32 = jnp.float32
P_SIZE = 64
N = 128
Q = 128
PER_GROUP = 16
GROUPS = 4
HEADS = GROUPS * PER_GROUP
GW = PER_GROUP * P_SIZE
TAIL = 16
LANES = 128
SMALL = 20 * 1024 * 1024
LARGE = 56 * 1024 * 1024


def dot(a, b):
    return jnp.dot(a, b, preferred_element_type=F32)


def dot_nt(a, b):
    return lax.dot_general(a, b, (((1,), (1,)), ((), ())), preferred_element_type=F32)


def dot_tn(a, b):
    return lax.dot_general(a, b, (((0,), (0,)), ((), ())), preferred_element_type=F32)


def split2(v):
    hi = v.astype(BF)
    return hi, (v - hi.astype(F32)).astype(BF)


def split3(v):
    hi = v.astype(BF)
    rest = v - hi.astype(F32)
    mid = rest.astype(BF)
    return hi, mid, (rest - mid.astype(F32)).astype(BF)


def iota(shape, dim):
    return lax.broadcasted_iota(jnp.int32, shape, dim)


def expander():
    return (iota((PER_GROUP, GW), 1) // P_SIZE == iota((PER_GROUP, GW), 0)).astype(F32).astype(BF)


def expand(v, e):
    return dot(jnp.concatenate(split2(v), axis=1), jnp.concatenate([e, e], axis=0))


def head_sums(v, e):
    hi, lo = split2(v)
    return dot_nt(hi, e) + dot_nt(lo, e)


def tri(lower):
    row, col = iota((Q, Q), 0), iota((Q, Q), 1)
    keep = row >= col if lower else row <= col
    return keep.astype(F32).astype(BF)


def scan_dot(t, v):
    a, b, c = split3(v)
    return dot(t, a) + dot(t, b) + dot(t, c)


def softplus(v):
    return jnp.maximum(v, 0.0) + jnp.log1p(jnp.exp(-jnp.abs(v)))


def front_kernel(
    idx, bias, rate, oth_h, li_h, x_h, dy_h, b_h, c_h, *refs
):
    blocks, (out, step_o, run_o, runt_o, w, li_oth, li_own, x, dy, b, c, sems) = refs[:-12], refs[-12:]
    chips = len(blocks) // 2
    pairs = [(oth_h, li_oth), (li_h, li_own), (b_h, b), (c_h, c), (x_h, x), (dy_h, dy)]
    for s, block in enumerate(blocks):
        chip = lax.rem(idx[1] // 2 - s % chips + chips, chips)
        core = lax.rem(idx[1] + s // chips, 2)
        pairs.insert(s, (block, w.at[2 * chip + core]))
    loads = [pltpu.make_async_copy(*pair, sems.at[k]) for k, pair in enumerate(pairs)]
    for load in loads:
        load.start()
    for load in loads[:-5]:
        load.wait()
    count, _, rows = w.shape
    per = count // 2
    step = bias[...]
    for k in range(per):
        step = step + dot_nt(li_oth[:, k * rows : (k + 1) * rows], w[(1 - idx[0]) * per + k])
    loads[-5].wait()
    for k in range(per):
        step = step + dot_nt(li_own[:, k * rows : (k + 1) * rows], w[idx[0] * per + k])
    step_o[...] = step
    running = scan_dot(tri(True), -rate[...] * softplus(step))
    runt_o[...] = jnp.swapaxes(running, 0, 1)
    e = expander()
    row = iota((TAIL, LANES), 0)
    _, total, _ = out.shape
    cuts = (total - TAIL) // (2 * N)
    shares = GW // (cuts * LANES)
    for load in loads[-4:]:
        load.wait()
    for g in range(GROUPS):
        r = running[:, g * PER_GROUP : (g + 1) * PER_GROUP]
        run_o[g] = r
        weight = expand(jnp.exp(r[Q - 1 :, :] - r), e)
        early = expand(jnp.exp(r), e)
        wide, slim = slice(g * GW, (g + 1) * GW), slice(g * N, (g + 1) * N)
        scaled = (x[:, wide].astype(F32) * weight).astype(BF)
        scaled_dy = (dy[:, wide].astype(F32) * early).astype(BF)
        piece = dot_tn(b[:, slim], scaled).astype(BF)
        jump = dot_tn(c[:, slim], scaled_dy).astype(BF)
        last = early[Q - 1 :, :]
        rest = last - last.astype(BF).astype(F32)
        for k in range(shares):
            tail = jnp.zeros((TAIL, LANES), F32)
            to = g * shares + k
            for i in range(cuts):
                lanes = slice((k * cuts + i) * LANES, (k * cuts + i + 1) * LANES)
                at = i * 2 * N
                out[to, at : at + N, :] = piece[:, lanes]
                out[to, at + N : at + 2 * N, :] = jump[:, lanes]
                tail = jnp.where(row == 2 * i, last[:, lanes], tail)
                tail = jnp.where(row == 2 * i + 1, rest[:, lanes], tail)
            out[to, total - TAIL :, :] = tail.astype(BF)


def local_kernel(x, dy, b, c, run, runt, direct_o, gdirect_o, gc_o, gb_o, gr_o):
    bg, cg = b[...], c[...]
    inner = dot_nt(cg, bg)
    inner2 = jnp.concatenate([inner, inner], axis=1)
    row, col = iota((Q, 2 * Q), 0), iota((Q, 2 * Q), 1)
    causal = row >= lax.rem(col, Q)
    first = iota((Q, 2 * P_SIZE), 1) < P_SIZE
    m1 = first.astype(F32).astype(BF)
    m2 = 1 - m1
    total = jnp.zeros((Q, Q), F32)
    for j in range(PER_GROUP // 2):
        lanes = slice(j * 2 * P_SIZE, (j + 1) * 2 * P_SIZE)
        xp, dyp = x[:, lanes], dy[:, lanes]
        xbd = jnp.concatenate([xp * m1, xp * m2], axis=0)
        diff = jnp.concatenate(
            [
                run[0, :, 2 * j + i : 2 * j + i + 1] - runt[2 * j + i : 2 * j + i + 1, :]
                for i in range(2)
            ],
            axis=1,
        )
        dec = jnp.exp(jnp.where(causal, diff, -1e30))
        ad = dot_nt(dyp, xbd) * dec
        total = total + ad[:, :Q] + ad[:, Q:]
        mix = (dec * inner2).astype(BF)
        direct_o[:, lanes] = dot(mix, xbd)
        both = dot_tn(mix, dyp)
        gdirect_o[:, lanes] = jnp.where(first, both[:Q], both[Q:])
    grad_inner = total.astype(BF)
    gc_o[...] = dot(grad_inner, bg)
    gb_o[...] = dot_tn(grad_inner, cg)
    gr_o[0] = head_sums(
        dy[...].astype(F32) * direct_o[...] - x[...].astype(F32) * gdirect_o[...], expander()
    )


def scan_kernel(msgs, out):
    count, total, _ = msgs.shape
    for i in range((total - TAIL) // (2 * N)):
        at = i * 2 * N

        def decay(k):
            tail = msgs[k, total - TAIL :, :].astype(F32)
            return tail[2 * i : 2 * i + 1, :] + tail[2 * i + 1 : 2 * i + 2, :]

        carry = jnp.zeros((N, LANES), F32)
        for k in range(count):
            out[k, at : at + N, :] = carry.astype(BF)
            if k < count - 1:
                carry = decay(k) * carry + msgs[k, at : at + N, :].astype(F32)
        back = jnp.zeros((N, LANES), F32)
        for k in range(count - 1, -1, -1):
            out[k, at + N : at + 2 * N, :] = back.astype(BF)
            if k > 0:
                back = decay(k) * back + msgs[k, at + N : at + 2 * N, :].astype(F32)


def states_of(states):
    shares, total, _ = states.shape
    starts = [(k, at) for k in range(shares) for at in range(0, total, 2 * N)]
    carry = jnp.concatenate([states[k, at : at + N, :] for k, at in starts], axis=1)
    back = jnp.concatenate([states[k, at + N : at + 2 * N, :] for k, at in starts], axis=1)
    return carry, back


def raw_kernel(states, x, dy, b, c, run, gr_i, step, rate, raw_o, rawt_o, gr):
    g = pl.program_id(0)
    e = expander()
    r = run[0]
    closing = r[Q - 1 :, :]
    carry, back = states_of(states)
    fore = head_sums(dy[...].astype(F32) * dot(c[...], carry), e)
    aft = jnp.exp(closing - r) * head_sums(x[...].astype(F32) * dot(b[...], back), e)
    both = jnp.sum(carry.astype(F32) * back.astype(F32), axis=0, keepdims=True)
    both = head_sums(jnp.broadcast_to(both, (8, GW)), e)[0:1, :]
    end = jnp.sum(aft, axis=0, keepdims=True) + jnp.exp(closing) * both
    gr[g] = (
        gr_i[0] + jnp.exp(r) * fore - aft + jnp.where(iota((Q, PER_GROUP), 0) == Q - 1, end, 0.0)
    )

    @pl.when(g == GROUPS - 1)
    def _():
        grad_running = jnp.concatenate([gr[k] for k in range(GROUPS)], axis=1)
        gate = scan_dot(tri(False), grad_running)
        raw = gate * -rate[...] * jax.nn.sigmoid(step[...])
        raw_o[...] = raw.astype(BF)
        rawt = jnp.swapaxes(raw, 0, 1).astype(BF)
        for k in range(rawt_o.shape[0]):
            rawt_o[k] = rawt


def finish_kernel(
    states, x, dy, b, c, run, skip, direct, gdirect, gc_i, gb_i, out_o, gx_o, gb_o, gc_o
):
    e = expander()
    r = run[0]
    weight = expand(jnp.exp(r[Q - 1 :, :] - r), e)
    early = expand(jnp.exp(r), e)
    gain = expand(jnp.broadcast_to(skip[0], (8, PER_GROUP)), e)[0:1, :]
    carry, back = states_of(states)
    xg, dyg = x[...].astype(F32), dy[...].astype(F32)
    out_o[...] = (direct[...] + early * dot(c[...], carry) + gain * xg).astype(BF)
    gx_o[...] = (gdirect[...] + weight * dot(b[...], back) + gain * dyg).astype(BF)
    gc_o[...] = (gc_i[...] + dot_nt((dyg * early).astype(BF), carry)).astype(BF)
    gb_o[...] = (gb_i[...] + dot_nt((xg * weight).astype(BF), back)).astype(BF)


def deal_kernel(idx, li_own, li_oth, *outs):
    count = len(outs)
    rows = outs[0].shape[1]
    per = count // 2
    for s, out in enumerate(outs):
        k = lax.rem(idx[1] + s, count)
        cols = pl.ds(pl.multiple_of(lax.rem(k, per) * rows, rows), rows)

        @pl.when(k // per == idx[0])
        def _():
            out[...] = li_own[:, cols]

        @pl.when(k // per != idx[0])
        def _():
            out[...] = li_oth[:, cols]


def rows_kernel(idx, rawt, *refs):
    out = refs[-1]
    count = len(refs) - 1
    total = jnp.zeros(out.shape, F32)
    for s in range(count):
        total = total + dot(rawt[lax.rem(idx[1] - s + count, count)], refs[s][...])
    out[...] = total.astype(out.dtype)


def add_kernel(*refs):
    a, b, c, d = (ref[...].astype(F32) for ref in refs[:-1])
    refs[-1][...] = ((a + c) + (b + d)).astype(refs[-1].dtype)


def input_kernel(idx, raw, raw_oth, w, w_oth, out):
    per, _, rows = w_oth.shape
    for k in range(per):
        out[:, k * rows : (k + 1) * rows] = (
            dot(raw[...], w[idx[0] * per + k]) + dot(raw_oth[...], w_oth[k])
        ).astype(BF)


SMEM_SPEC = pl.BlockSpec(memory_space=pltpu.SMEM)
VMEM_SPEC = pl.BlockSpec(memory_space=pltpu.VMEM)


def sds(shape, dtype):
    return jax.ShapeDtypeStruct(shape, dtype)


def call(kernel, name, outs, *args, scratch=(), scalars=0, vmem=SMALL):
    params = pltpu.CompilerParams(vmem_limit_bytes=vmem)
    return pl.pallas_call(
        kernel,
        out_shape=outs,
        in_specs=[SMEM_SPEC] * scalars + [VMEM_SPEC] * (len(args) - scalars),
        out_specs=jax.tree.map(lambda _: VMEM_SPEC, outs),
        scratch_shapes=list(scratch),
        compiler_params=params,
        name=name,
    )(*args)


def columns(width, first=0):
    return pl.BlockSpec((Q, width), lambda g: (0, g + first))


def heads_of(first=0):
    return pl.BlockSpec((1, Q, PER_GROUP), lambda g: (g + first, 0, 0))


def shards(
    layer_input, w_step, step_bias, decay_rate, ssm_input, b_input, c_input, skip_gain, grad_y
):
    dp, ctx = lax.axis_size("dp"), lax.axis_size("ctx")
    nz = GROUPS
    ny = ctx // nz
    me = lax.axis_index("head")
    idx = jnp.stack([me, lax.axis_index("dp")]).astype(jnp.int32)
    swap = [(0, 1), (1, 0)]
    params = pltpu.CompilerParams(vmem_limit_bytes=LARGE)

    def z_shift(v, s):
        pairs = [(y * nz + k, y * nz + (k + s) % nz) for y in range(ny) for k in range(nz)]
        return lax.ppermute(v, "ctx", pairs)

    def y_shift(v, s):
        pairs = [(y * nz + k, (y + s) % ny * nz + k) for y in range(ny) for k in range(nz)]
        return lax.ppermute(v, "ctx", pairs)

    li = layer_input[0]
    x, dy, b, c = ssm_input[0], grad_y[0], b_input[0], c_input[0]
    half = li.shape[1]
    rows = w_step.shape[0]
    per = half // rows
    bias, rate = step_bias.reshape(1, HEADS), decay_rate.reshape(1, HEADS)
    skip = skip_gain.reshape(GROUPS, 1, PER_GROUP)

    li_oth = lax.ppermute(li, "head", swap)
    chips = dp // 2
    mine = [w_step.T]
    mine += [
        lax.ppermute(mine[0], "dp", [(k, (k + 2 * s) % dp) for k in range(dp)])
        for s in range(1, chips)
    ]
    w_blocks = mine + [lax.ppermute(v, "dp", [(k, k ^ 1) for k in range(dp)]) for v in mine]
    cuts = GROUPS * GW // (ctx * LANES)
    shares = GW // (cuts * LANES)
    total = cuts * 2 * N
    sent, step, run, runt, w = pl.pallas_call(
        front_kernel,
        out_shape=[
            sds((ctx, total + TAIL, LANES), BF),
            sds((Q, HEADS), F32),
            sds((GROUPS, Q, PER_GROUP), F32),
            sds((HEADS, Q), F32),
            sds((dp, HEADS, rows), BF),
        ],
        in_specs=[SMEM_SPEC] + [VMEM_SPEC] * 2 + [pl.BlockSpec(memory_space=pl.ANY)] * (6 + dp),
        out_specs=[VMEM_SPEC] * 5,
        scratch_shapes=[
            pltpu.VMEM((Q, half), BF),
            pltpu.VMEM((Q, half), BF),
            pltpu.VMEM((Q, GROUPS * GW), BF),
            pltpu.VMEM((Q, GROUPS * GW), BF),
            pltpu.VMEM((Q, GROUPS * N), BF),
            pltpu.VMEM((Q, GROUPS * N), BF),
            pltpu.SemaphoreType.DMA((6 + dp,)),
        ],
        compiler_params=params,
        name="front",
    )(idx, bias, rate, li_oth, li, x, dy, b, c, *w_blocks)
    got = lax.all_to_all(sent, "ctx", 0, 0, tiled=True)

    w_oth = lax.ppermute(lax.dynamic_slice_in_dim(w, (1 - me) * per, per, 0), "head", swap)
    dealt = call(deal_kernel, "deal", [sds((Q, rows), BF)] * dp, idx, li, li_oth, scalars=1)
    li_rows = [dealt[0]] + [
        lax.ppermute(dealt[s], "dp", [(k, (k + s) % dp) for k in range(dp)]) for s in range(1, dp)
    ]

    direct, gdirect, gc, gb, gr = pl.pallas_call(
        local_kernel,
        grid=(GROUPS,),
        out_shape=[
            sds((Q, GROUPS * GW), F32),
            sds((Q, GROUPS * GW), F32),
            sds((Q, GROUPS * N), F32),
            sds((Q, GROUPS * N), F32),
            sds((GROUPS, Q, PER_GROUP), F32),
        ],
        in_specs=[
            columns(GW), columns(GW), columns(N), columns(N), heads_of(),
            pl.BlockSpec((PER_GROUP, Q), lambda g: (g, 0)),
        ],
        out_specs=[columns(GW), columns(GW), columns(N), columns(N), heads_of()],
        compiler_params=params,
        cost_estimate=pl.CostEstimate(
            flops=4_000_000_000, bytes_accessed=12_000_000, transcendentals=1_100_000
        ),
        name="local",
    )(x, dy, b, c, run, runt)

    back = call(scan_kernel, "scan", sds((ctx, total, LANES), BF), got)
    states = lax.all_to_all(back, "ctx", 0, 0, tiled=True)
    states, li_rows, skip = lax.optimization_barrier((states, li_rows, skip))
    state_spec = pl.BlockSpec((shares, total, LANES), lambda g: (g, 0, 0))
    whole = lambda *shape: pl.BlockSpec(shape, lambda g: (0,) * len(shape))

    raw, rawt = pl.pallas_call(
        raw_kernel,
        grid=(GROUPS,),
        out_shape=[sds((Q, HEADS), BF), sds((dp, HEADS, Q), BF)],
        in_specs=[
            state_spec, columns(GW), columns(GW), columns(N), columns(N), heads_of(), heads_of(),
            whole(Q, HEADS), whole(1, HEADS),
        ],
        out_specs=[whole(Q, HEADS), whole(dp, HEADS, Q)],
        scratch_shapes=[pltpu.VMEM((GROUPS, Q, PER_GROUP), F32)],
        compiler_params=params,
        name="raw",
    )(states, x, dy, b, c, run, gr, step, rate)

    outs = pl.pallas_call(
        finish_kernel,
        grid=(GROUPS,),
        out_shape=[
            sds((Q, GROUPS * GW), BF),
            sds((Q, GROUPS * GW), BF),
            sds((Q, GROUPS * N), BF),
            sds((Q, GROUPS * N), BF),
        ],
        in_specs=[
            state_spec, columns(GW), columns(GW), columns(N), columns(N), heads_of(),
            pl.BlockSpec((1, 1, PER_GROUP), lambda g: (g, 0, 0)),
            columns(GW), columns(GW), columns(N), columns(N),
        ],
        out_specs=[columns(GW), columns(GW), columns(N), columns(N)],
        compiler_params=params,
        cost_estimate=pl.CostEstimate(
            flops=4_000_000_000, bytes_accessed=12_000_000, transcendentals=200_000
        ),
        name="finish",
    )(states, x, dy, b, c, run, skip, direct, gdirect, gc, gb)

    raw_oth = lax.ppermute(raw, "head", swap)
    rawt = lax.all_to_all(rawt, "dp", 0, 0, tiled=True)
    rawt, raw_oth = lax.optimization_barrier((rawt, raw_oth))
    share = call(rows_kernel, "rows", sds((HEADS, rows), BF), idx, rawt, *li_rows, scalars=1, vmem=LARGE)
    near = [z_shift(share, s) for s in range(1, nz)]
    near, outs = lax.optimization_barrier((near, outs))
    output, grad_x, grad_b, grad_c = outs
    share = call(add_kernel, "add_z", sds((HEADS, rows), BF), share, *near)
    grad_input = call(
        input_kernel, "input", sds((Q, half), BF), idx, raw, raw_oth, w, w_oth, scalars=1
    )
    near = [y_shift(share, s) for s in range(1, ny)]
    near, grad_input = lax.optimization_barrier((near, grad_input))
    grad_w = call(add_kernel, "add_y", sds((HEADS, rows), F32), share, *near)
    return output[None], grad_x[None], grad_b[None], grad_c[None], grad_input[None], grad_w.T


def solution(mesh):
    tokens = P("dp", "ctx", "head")
    in_specs = (
        tokens, P("dp", "head"), P("head"), P("head"), tokens, tokens, tokens, P("head"), tokens,
    )
    out_specs = (tokens, tokens, tokens, tokens, tokens, P("dp", "head"))
    return jax.shard_map(shards, mesh=mesh, in_specs=in_specs, out_specs=out_specs, check_vma=False)
```

```python
import jax
import jax.numpy as jnp
from jax import lax
from jax.experimental import pallas as pl
from jax.experimental.pallas import tpu as pltpu
from jax.sharding import PartitionSpec as P

BF = jnp.bfloat16
F32 = jnp.float32
P_SIZE = 64
N = 128
Q = 128
PER_GROUP = 16
GROUPS = 4
HEADS = GROUPS * PER_GROUP
GW = PER_GROUP * P_SIZE
TAIL = 16
LANES = 128
SMALL = 20 * 1024 * 1024
LARGE = 56 * 1024 * 1024


def dot(a, b):
    return jnp.dot(a, b, preferred_element_type=F32)


def dot_nt(a, b):
    return lax.dot_general(a, b, (((1,), (1,)), ((), ())), preferred_element_type=F32)


def dot_tn(a, b):
    return lax.dot_general(a, b, (((0,), (0,)), ((), ())), preferred_element_type=F32)


def split2(v):
    hi = v.astype(BF)
    return hi, (v - hi.astype(F32)).astype(BF)


def split3(v):
    hi = v.astype(BF)
    rest = v - hi.astype(F32)
    mid = rest.astype(BF)
    return hi, mid, (rest - mid.astype(F32)).astype(BF)


def iota(shape, dim):
    return lax.broadcasted_iota(jnp.int32, shape, dim)


def expander():
    return (iota((PER_GROUP, GW), 1) // P_SIZE == iota((PER_GROUP, GW), 0)).astype(F32).astype(BF)


def expand(v, e):
    return dot(jnp.concatenate(split2(v), axis=1), jnp.concatenate([e, e], axis=0))


def head_sums(v, e):
    hi, lo = split2(v)
    return dot_nt(hi, e) + dot_nt(lo, e)


def tri(lower):
    row, col = iota((Q, Q), 0), iota((Q, Q), 1)
    keep = row >= col if lower else row <= col
    return keep.astype(F32).astype(BF)


def scan_dot(t, v):
    a, b, c = split3(v)
    return dot(t, a) + dot(t, b) + dot(t, c)


def softplus(v):
    return jnp.maximum(v, 0.0) + jnp.log1p(jnp.exp(-jnp.abs(v)))


def front_kernel(
    idx, bias, rate, oth_h, li_h, x_h, dy_h, b_h, c_h, *refs
):
    blocks, (out, step_o, run_o, runt_o, w, li_oth, li_own, x, dy, b, c, sems) = refs[:-12], refs[-12:]
    chips = len(blocks) // 2
    pairs = [(oth_h, li_oth), (li_h, li_own), (b_h, b), (c_h, c), (x_h, x), (dy_h, dy)]
    for s, block in enumerate(blocks):
        chip = lax.rem(idx[1] // 2 - s % chips + chips, chips)
        core = lax.rem(idx[1] + s // chips, 2)
        pairs.insert(s, (block, w.at[2 * chip + core]))
    loads = [pltpu.make_async_copy(*pair, sems.at[k]) for k, pair in enumerate(pairs)]
    for load in loads:
        load.start()
    for load in loads[:-5]:
        load.wait()
    count, _, rows = w.shape
    per = count // 2
    step = bias[...]
    for k in range(per):
        step = step + dot_nt(li_oth[:, k * rows : (k + 1) * rows], w[(1 - idx[0]) * per + k])
    loads[-5].wait()
    for k in range(per):
        step = step + dot_nt(li_own[:, k * rows : (k + 1) * rows], w[idx[0] * per + k])
    step_o[...] = step
    running = scan_dot(tri(True), -rate[...] * softplus(step))
    runt_o[...] = jnp.swapaxes(running, 0, 1)
    e = expander()
    row = iota((TAIL, LANES), 0)
    _, total, _ = out.shape
    cuts = (total - TAIL) // (2 * N)
    shares = GW // (cuts * LANES)
    for load in loads[-4:]:
        load.wait()
    for g in range(GROUPS):
        r = running[:, g * PER_GROUP : (g + 1) * PER_GROUP]
        run_o[g] = r
        weight = expand(jnp.exp(r[Q - 1 :, :] - r), e)
        early = expand(jnp.exp(r), e)
        wide, slim = slice(g * GW, (g + 1) * GW), slice(g * N, (g + 1) * N)
        scaled = (x[:, wide].astype(F32) * weight).astype(BF)
        scaled_dy = (dy[:, wide].astype(F32) * early).astype(BF)
        piece = dot_tn(b[:, slim], scaled).astype(BF)
        jump = dot_tn(c[:, slim], scaled_dy).astype(BF)
        last = early[Q - 1 :, :]
        rest = last - last.astype(BF).astype(F32)
        for k in range(shares):
            tail = jnp.zeros((TAIL, LANES), F32)
            to = g * shares + k
            for i in range(cuts):
                lanes = slice((k * cuts + i) * LANES, (k * cuts + i + 1) * LANES)
                at = i * 2 * N
                out[to, at : at + N, :] = piece[:, lanes]
                out[to, at + N : at + 2 * N, :] = jump[:, lanes]
                tail = jnp.where(row == 2 * i, last[:, lanes], tail)
                tail = jnp.where(row == 2 * i + 1, rest[:, lanes], tail)
            out[to, total - TAIL :, :] = tail.astype(BF)


def local_kernel(x, dy, b, c, run, runt, direct_o, gdirect_o, gc_o, gb_o, gr_o):
    bg, cg = b[...], c[...]
    inner = dot_nt(cg, bg)
    inner2 = jnp.concatenate([inner, inner], axis=1)
    row, col = iota((Q, 2 * Q), 0), iota((Q, 2 * Q), 1)
    causal = row >= lax.rem(col, Q)
    first = iota((Q, 2 * P_SIZE), 1) < P_SIZE
    m1 = first.astype(F32).astype(BF)
    m2 = 1 - m1
    total = jnp.zeros((Q, Q), F32)
    for j in range(PER_GROUP // 2):
        lanes = slice(j * 2 * P_SIZE, (j + 1) * 2 * P_SIZE)
        xp, dyp = x[:, lanes], dy[:, lanes]
        xbd = jnp.concatenate([xp * m1, xp * m2], axis=0)
        diff = jnp.concatenate(
            [
                run[0, :, 2 * j + i : 2 * j + i + 1] - runt[2 * j + i : 2 * j + i + 1, :]
                for i in range(2)
            ],
            axis=1,
        )
        dec = jnp.exp(jnp.where(causal, diff, -1e30))
        ad = dot_nt(dyp, xbd) * dec
        total = total + ad[:, :Q] + ad[:, Q:]
        mix = (dec * inner2).astype(BF)
        direct_o[:, lanes] = dot(mix, xbd)
        both = dot_tn(mix, dyp)
        gdirect_o[:, lanes] = jnp.where(first, both[:Q], both[Q:])
    grad_inner = total.astype(BF)
    gc_o[...] = dot(grad_inner, bg)
    gb_o[...] = dot_tn(grad_inner, cg)
    gr_o[0] = head_sums(
        dy[...].astype(F32) * direct_o[...] - x[...].astype(F32) * gdirect_o[...], expander()
    )


def scan_kernel(msgs, out):
    count, total, _ = msgs.shape
    for i in range((total - TAIL) // (2 * N)):
        at = i * 2 * N

        def decay(k):
            tail = msgs[k, total - TAIL :, :].astype(F32)
            return tail[2 * i : 2 * i + 1, :] + tail[2 * i + 1 : 2 * i + 2, :]

        carry = jnp.zeros((N, LANES), F32)
        for k in range(count):
            out[k, at : at + N, :] = carry.astype(BF)
            if k < count - 1:
                carry = decay(k) * carry + msgs[k, at : at + N, :].astype(F32)
        back = jnp.zeros((N, LANES), F32)
        for k in range(count - 1, -1, -1):
            out[k, at + N : at + 2 * N, :] = back.astype(BF)
            if k > 0:
                back = decay(k) * back + msgs[k, at + N : at + 2 * N, :].astype(F32)


def states_of(states):
    shares, total, _ = states.shape
    starts = [(k, at) for k in range(shares) for at in range(0, total, 2 * N)]
    carry = jnp.concatenate([states[k, at : at + N, :] for k, at in starts], axis=1)
    back = jnp.concatenate([states[k, at + N : at + 2 * N, :] for k, at in starts], axis=1)
    return carry, back


def raw_kernel(states, x, dy, b, c, run, gr_i, step, rate, raw_o, rawt_o, gr):
    g = pl.program_id(0)
    e = expander()
    r = run[0]
    closing = r[Q - 1 :, :]
    carry, back = states_of(states)
    fore = head_sums(dy[...].astype(F32) * dot(c[...], carry), e)
    aft = jnp.exp(closing - r) * head_sums(x[...].astype(F32) * dot(b[...], back), e)
    both = jnp.sum(carry.astype(F32) * back.astype(F32), axis=0, keepdims=True)
    both = head_sums(jnp.broadcast_to(both, (8, GW)), e)[0:1, :]
    end = jnp.sum(aft, axis=0, keepdims=True) + jnp.exp(closing) * both
    gr[g] = (
        gr_i[0] + jnp.exp(r) * fore - aft + jnp.where(iota((Q, PER_GROUP), 0) == Q - 1, end, 0.0)
    )

    @pl.when(g == GROUPS - 1)
    def _():
        grad_running = jnp.concatenate([gr[k] for k in range(GROUPS)], axis=1)
        gate = scan_dot(tri(False), grad_running)
        raw = gate * -rate[...] * jax.nn.sigmoid(step[...])
        raw_o[...] = raw.astype(BF)
        rawt = jnp.swapaxes(raw, 0, 1).astype(BF)
        for k in range(rawt_o.shape[0]):
            rawt_o[k] = rawt


def finish_kernel(
    states, x, dy, b, c, run, skip, direct, gdirect, gc_i, gb_i, out_o, gx_o, gb_o, gc_o
):
    e = expander()
    r = run[0]
    weight = expand(jnp.exp(r[Q - 1 :, :] - r), e)
    early = expand(jnp.exp(r), e)
    gain = expand(jnp.broadcast_to(skip[0], (8, PER_GROUP)), e)[0:1, :]
    carry, back = states_of(states)
    xg, dyg = x[...].astype(F32), dy[...].astype(F32)
    out_o[...] = (direct[...] + early * dot(c[...], carry) + gain * xg).astype(BF)
    gx_o[...] = (gdirect[...] + weight * dot(b[...], back) + gain * dyg).astype(BF)
    gc_o[...] = (gc_i[...] + dot_nt((dyg * early).astype(BF), carry)).astype(BF)
    gb_o[...] = (gb_i[...] + dot_nt((xg * weight).astype(BF), back)).astype(BF)


def deal_kernel(idx, li_own, li_oth, *outs):
    count = len(outs)
    rows = outs[0].shape[1]
    per = count // 2
    for s, out in enumerate(outs):
        k = lax.rem(idx[1] + s, count)
        cols = pl.ds(pl.multiple_of(lax.rem(k, per) * rows, rows), rows)

        @pl.when(k // per == idx[0])
        def _():
            out[...] = li_own[:, cols]

        @pl.when(k // per != idx[0])
        def _():
            out[...] = li_oth[:, cols]


def rows_kernel(idx, rawt, *refs):
    out = refs[-1]
    count = len(refs) - 1
    total = jnp.zeros(out.shape, F32)
    for s in range(count):
        total = total + dot(rawt[lax.rem(idx[1] - s + count, count)], refs[s][...])
    out[...] = total.astype(out.dtype)


def add_kernel(*refs):
    a, b, c, d = (ref[...].astype(F32) for ref in refs[:-1])
    refs[-1][...] = ((a + c) + (b + d)).astype(refs[-1].dtype)


def input_kernel(idx, raw, raw_oth, w, w_oth, out):
    per, _, rows = w_oth.shape
    for k in range(per):
        out[:, k * rows : (k + 1) * rows] = (
            dot(raw[...], w[idx[0] * per + k]) + dot(raw_oth[...], w_oth[k])
        ).astype(BF)


SMEM_SPEC = pl.BlockSpec(memory_space=pltpu.SMEM)
VMEM_SPEC = pl.BlockSpec(memory_space=pltpu.VMEM)


def sds(shape, dtype):
    return jax.ShapeDtypeStruct(shape, dtype)


def call(kernel, name, outs, *args, scratch=(), scalars=0, vmem=SMALL):
    params = pltpu.CompilerParams(vmem_limit_bytes=vmem)
    return pl.pallas_call(
        kernel,
        out_shape=outs,
        in_specs=[SMEM_SPEC] * scalars + [VMEM_SPEC] * (len(args) - scalars),
        out_specs=jax.tree.map(lambda _: VMEM_SPEC, outs),
        scratch_shapes=list(scratch),
        compiler_params=params,
        name=name,
    )(*args)


def columns(width, first=0):
    return pl.BlockSpec((Q, width), lambda g: (0, g + first))


def heads_of(first=0):
    return pl.BlockSpec((1, Q, PER_GROUP), lambda g: (g + first, 0, 0))


def shards(
    layer_input, w_step, step_bias, decay_rate, ssm_input, b_input, c_input, skip_gain, grad_y
):
    dp, ctx = lax.axis_size("dp"), lax.axis_size("ctx")
    nz = GROUPS
    ny = ctx // nz
    me = lax.axis_index("head")
    idx = jnp.stack([me, lax.axis_index("dp")]).astype(jnp.int32)
    swap = [(0, 1), (1, 0)]
    params = pltpu.CompilerParams(vmem_limit_bytes=LARGE)

    def z_shift(v, s):
        pairs = [(y * nz + k, y * nz + (k + s) % nz) for y in range(ny) for k in range(nz)]
        return lax.ppermute(v, "ctx", pairs)

    def y_shift(v, s):
        pairs = [(y * nz + k, (y + s) % ny * nz + k) for y in range(ny) for k in range(nz)]
        return lax.ppermute(v, "ctx", pairs)

    li = layer_input[0]
    x, dy, b, c = ssm_input[0], grad_y[0], b_input[0], c_input[0]
    half = li.shape[1]
    rows = w_step.shape[0]
    per = half // rows
    bias, rate = step_bias.reshape(1, HEADS), decay_rate.reshape(1, HEADS)
    skip = skip_gain.reshape(GROUPS, 1, PER_GROUP)

    li_oth = lax.ppermute(li, "head", swap)
    chips = dp // 2
    mine = [w_step.T]
    mine += [
        lax.ppermute(mine[0], "dp", [(k, (k + 2 * s) % dp) for k in range(dp)])
        for s in range(1, chips)
    ]
    w_blocks = mine + [lax.ppermute(v, "dp", [(k, k ^ 1) for k in range(dp)]) for v in mine]
    cuts = GROUPS * GW // (ctx * LANES)
    shares = GW // (cuts * LANES)
    total = cuts * 2 * N
    sent, step, run, runt, w = pl.pallas_call(
        front_kernel,
        out_shape=[
            sds((ctx, total + TAIL, LANES), BF),
            sds((Q, HEADS), F32),
            sds((GROUPS, Q, PER_GROUP), F32),
            sds((HEADS, Q), F32),
            sds((dp, HEADS, rows), BF),
        ],
        in_specs=[SMEM_SPEC] + [VMEM_SPEC] * 2 + [pl.BlockSpec(memory_space=pl.ANY)] * (6 + dp),
        out_specs=[VMEM_SPEC] * 5,
        scratch_shapes=[
            pltpu.VMEM((Q, half), BF),
            pltpu.VMEM((Q, half), BF),
            pltpu.VMEM((Q, GROUPS * GW), BF),
            pltpu.VMEM((Q, GROUPS * GW), BF),
            pltpu.VMEM((Q, GROUPS * N), BF),
            pltpu.VMEM((Q, GROUPS * N), BF),
            pltpu.SemaphoreType.DMA((6 + dp,)),
        ],
        compiler_params=params,
        name="front",
    )(idx, bias, rate, li_oth, li, x, dy, b, c, *w_blocks)
    got = lax.all_to_all(sent, "ctx", 0, 0, tiled=True)

    w_oth = lax.ppermute(lax.dynamic_slice_in_dim(w, (1 - me) * per, per, 0), "head", swap)
    dealt = call(deal_kernel, "deal", [sds((Q, rows), BF)] * dp, idx, li, li_oth, scalars=1)
    li_rows = [dealt[0]] + [
        lax.ppermute(dealt[s], "dp", [(k, (k + s) % dp) for k in range(dp)]) for s in range(1, dp)
    ]

    direct, gdirect, gc, gb, gr = pl.pallas_call(
        local_kernel,
        grid=(GROUPS,),
        out_shape=[
            sds((Q, GROUPS * GW), F32),
            sds((Q, GROUPS * GW), F32),
            sds((Q, GROUPS * N), F32),
            sds((Q, GROUPS * N), F32),
            sds((GROUPS, Q, PER_GROUP), F32),
        ],
        in_specs=[
            columns(GW), columns(GW), columns(N), columns(N), heads_of(),
            pl.BlockSpec((PER_GROUP, Q), lambda g: (g, 0)),
        ],
        out_specs=[columns(GW), columns(GW), columns(N), columns(N), heads_of()],
        compiler_params=params,
        cost_estimate=pl.CostEstimate(
            flops=4_000_000_000, bytes_accessed=12_000_000, transcendentals=1_100_000
        ),
        name="local",
    )(x, dy, b, c, run, runt)

    back = call(scan_kernel, "scan", sds((ctx, total, LANES), BF), got)
    states = lax.all_to_all(back, "ctx", 0, 0, tiled=True)
    states, li_rows, skip = lax.optimization_barrier((states, li_rows, skip))
    state_spec = pl.BlockSpec((shares, total, LANES), lambda g: (g, 0, 0))
    whole = lambda *shape: pl.BlockSpec(shape, lambda g: (0,) * len(shape))

    raw, rawt = pl.pallas_call(
        raw_kernel,
        grid=(GROUPS,),
        out_shape=[sds((Q, HEADS), BF), sds((dp, HEADS, Q), BF)],
        in_specs=[
            state_spec, columns(GW), columns(GW), columns(N), columns(N), heads_of(), heads_of(),
            whole(Q, HEADS), whole(1, HEADS),
        ],
        out_specs=[whole(Q, HEADS), whole(dp, HEADS, Q)],
        scratch_shapes=[pltpu.VMEM((GROUPS, Q, PER_GROUP), F32)],
        compiler_params=params,
        name="raw",
    )(states, x, dy, b, c, run, gr, step, rate)

    outs = pl.pallas_call(
        finish_kernel,
        grid=(GROUPS,),
        out_shape=[
            sds((Q, GROUPS * GW), BF),
            sds((Q, GROUPS * GW), BF),
            sds((Q, GROUPS * N), BF),
            sds((Q, GROUPS * N), BF),
        ],
        in_specs=[
            state_spec, columns(GW), columns(GW), columns(N), columns(N), heads_of(),
            pl.BlockSpec((1, 1, PER_GROUP), lambda g: (g, 0, 0)),
            columns(GW), columns(GW), columns(N), columns(N),
        ],
        out_specs=[columns(GW), columns(GW), columns(N), columns(N)],
        compiler_params=params,
        cost_estimate=pl.CostEstimate(
            flops=4_000_000_000, bytes_accessed=12_000_000, transcendentals=200_000
        ),
        name="finish",
    )(states, x, dy, b, c, run, skip, direct, gdirect, gc, gb)

    raw_oth = lax.ppermute(raw, "head", swap)
    rawt = lax.all_to_all(rawt, "dp", 0, 0, tiled=True)
    rawt, raw_oth = lax.optimization_barrier((rawt, raw_oth))
    share = call(rows_kernel, "rows", sds((HEADS, rows), BF), idx, rawt, *li_rows, scalars=1, vmem=SMALL)
    near = [z_shift(share, s) for s in range(1, nz)]
    near, outs = lax.optimization_barrier((near, outs))
    output, grad_x, grad_b, grad_c = outs
    share = call(add_kernel, "add_z", sds((HEADS, rows), BF), share, *near)
    grad_input = call(
        input_kernel, "input", sds((Q, half), BF), idx, raw, raw_oth, w, w_oth, scalars=1
    )
    near = [y_shift(share, s) for s in range(1, ny)]
    near, grad_input = lax.optimization_barrier((near, grad_input))
    grad_w = call(add_kernel, "add_y", sds((HEADS, rows), F32), share, *near)
    return output[None], grad_x[None], grad_b[None], grad_c[None], grad_input[None], grad_w.T


def solution(mesh):
    tokens = P("dp", "ctx", "head")
    in_specs = (
        tokens, P("dp", "head"), P("head"), P("head"), tokens, tokens, tokens, P("head"), tokens,
    )
    out_specs = (tokens, tokens, tokens, tokens, tokens, P("dp", "head"))
    return jax.shard_map(shards, mesh=mesh, in_specs=in_specs, out_specs=out_specs, check_vma=False)
```
